32 devices in a mesh: member: 4 (over y, x), tile: 8 (over z, core).
Axes of the slice: x: 2, y: 2, z: 4, core: 2. Of those that a mesh axis runs over, the one named last changes fastest.
Arguments:
- density: float32 [4, 6, 128, 128], P('member', None, 'tile'), may hold values from 0.05 to 5
- scaling: float32 [4, 6, 128, 128], P('member', None, 'tile'), may hold values from 0.2 to 5
- member_weights: float32 [4], P('member'), may hold values from 0.5 to 11
- seams: int32 [3, 4, 6], replicated, may hold values from 0 to 5, as said below
Outputs:
- new_scaling: float32 [4, 6, 128, 128], P('member', None, 'tile')
- dual_scaling: float32 [4, 6, 128, 128], P('member', None, 'tile')
- barycenter: float32 [6, 128, 128], P(None, 'tile')
The draws below stay inside these ranges and needn't reach their ends.
Inputs may be any that keep to these rules, and one draw needn't show every extreme that they name: Edges are numbered 0 first row, 1 last row, 2 first column, 3 last column. The table describes the six faces of a cube, each face's frame turned or mirrored: seams[0, e, f] is the face across edge e of face f, seams[1, e, f] the edge of that face which meets it, and the relation is symmetric; seams[2, e, f] is 1 where positions along the seam run opposite ways on the two faces, and the same from both sides.
All inputs are finite; a program needn't handle non-finite values.
Results may differ from the reference program's by a relative error of at most 0.00007.
Values sent between devices are 32-bit elements; how exact they have to be, the bound alone decides.
A program may use at most 64 MiB of HBM per device.

```python
import math
import jax
import jax.numpy as jnp
from jax import lax

FACES = 6
STEPS = 4
MEMBERS = 4
SIDE = 128


def draw_seams(key, part):
    key = jax.random.fold_in(key, 5)
    normal = jnp.array([[1, 0, 0], [-1, 0, 0], [0, 1, 0], [0, -1, 0], [0, 0, 1], [0, 0, -1]], jnp.int32)
    across = jnp.array([[0, 1, 0], [0, 0, 1], [0, 0, 1], [1, 0, 0], [1, 0, 0], [0, 1, 0]], jnp.int32)
    downward = jnp.array([[0, 0, 1], [0, 1, 0], [1, 0, 0], [0, 0, 1], [0, 1, 0], [1, 0, 0]], jnp.int32)
    symmetry = jax.random.randint(jax.random.fold_in(key, 1), (6,), 0, 8).astype(jnp.int32)
    swapped = (symmetry % 2 == 1)[:, None]
    sign_a = (1 - 2 * (symmetry // 2 % 2))[:, None]
    sign_b = (1 - 2 * (symmetry // 4 % 2))[:, None]
    axis_a = sign_a * jnp.where(swapped, downward, across)
    axis_b = sign_b * jnp.where(swapped, across, downward)
    order = jax.random.permutation(jax.random.fold_in(key, 2), 6).astype(jnp.int32)
    normal = jnp.zeros((6, 3), jnp.int32).at[order].set(normal)
    axis_a = jnp.zeros((6, 3), jnp.int32).at[order].set(axis_a)
    axis_b = jnp.zeros((6, 3), jnp.int32).at[order].set(axis_b)
    outward = jnp.stack([-axis_b, axis_b, -axis_a, axis_a], axis=1)
    along = jnp.stack([axis_a, axis_a, axis_b, axis_b], axis=1)
    match_face = jnp.all(outward[:, :, None, :] == normal[None, None, :, :], axis=-1).astype(jnp.int32)
    face = jnp.sum(match_face * jnp.arange(6, dtype=jnp.int32)[None, None, :], axis=-1).astype(jnp.int32)
    other_out = outward[face]
    meeting = jnp.all(other_out == normal[:, None, None, :], axis=-1).astype(jnp.int32)
    edge = jnp.sum(meeting * jnp.arange(4, dtype=jnp.int32)[None, None, :], axis=-1).astype(jnp.int32)
    other_along = along[face, edge]
    flip = (jnp.sum(along * other_along, axis=-1) < 0).astype(jnp.int32)
    return jnp.stack([face.T, edge.T, flip.T]).astype(jnp.int32)


def draw_member_weights(key, part):
    key = jax.random.fold_in(key, 3)
    rising = 1.0 + 2.0 * jnp.arange(MEMBERS, dtype=jnp.float32) / (MEMBERS - 1)
    return rising * jax.random.uniform(key, (MEMBERS,), jnp.float32, 0.6, 1.4)


def steps_of(stream_key, extent, shards, low, largest):
    factor_of, own = 1.0, jax.random.fold_in(stream_key, 6)
    for axis_at, shards_of in shards:
        steps = jnp.exp(jax.random.uniform(jax.random.fold_in(own, axis_at), (shards_of,), jnp.float32, low / len(shards), largest / len(shards)))
        factor_of = factor_of * jnp.repeat(steps, extent[axis_at] // shards_of).reshape([-1 if axis == axis_at else 1 for axis in range(len(extent))])
    return factor_of


def setup_inputs(seed: int = 0) -> dict:
    keys = jax.random.split(jax.random.key(seed), 5)
    return {
        "density": jnp.clip(jnp.exp(math.log(5.0) - 4.6051702 * jax.random.uniform(keys[0], (MEMBERS, FACES, SIDE, SIDE), jnp.float32) ** steps_of(keys[0], (MEMBERS, FACES, SIDE, SIDE), ((0, 4), (2, 8)), -0.2, 0.2)), 0.05, 5.0),
        "scaling": jnp.clip(jnp.exp(math.log(5.0) - 3.218876 * jax.random.uniform(keys[1], (MEMBERS, FACES, SIDE, SIDE), jnp.float32) ** steps_of(keys[1], (MEMBERS, FACES, SIDE, SIDE), ((0, 4), (2, 8)), -0.2, 0.2)), 0.2, 5.0),
        "member_weights": draw_member_weights(jax.random.fold_in(keys[4], 71), 0),
        "seams": draw_seams(jax.random.fold_in(keys[4], 71), 0),
    }


KAPPA = 0.24


def ghost_lines(field, seams):
    edges = jnp.stack([field[:, 0, :], field[:, -1, :], field[:, :, 0], field[:, :, -1]], axis=1)
    result = []
    for edge_id in range(4):
        taken = edges[seams[0, edge_id], seams[1, edge_id]]
        result.append(jnp.where((seams[2, edge_id] == 1)[:, None], taken[:, ::-1], taken))
    return result


def diffuse(field, seams):
    upper, lower, left, right = ghost_lines(field, seams)
    widened = jnp.concatenate([upper[:, None, :], field, lower[:, None, :]], axis=1)
    vertical = widened[:, :-2, :] + widened[:, 2:, :]
    lateral = jnp.concatenate([left[:, :, None], field[:, :, :-1]], axis=2) + jnp.concatenate([field[:, :, 1:], right[:, :, None]], axis=2)
    return field + KAPPA * ((vertical + lateral) - 4.0 * field)


def reference(density, scaling, member_weights, seams):
    def kernel(field):
        for counter in range(STEPS):
            field = diffuse(field, seams)
        return field

    def member_pass(pair_args):
        member_density, member_scaling = pair_args
        dual_field = member_density / kernel(member_scaling)
        marginal_field = member_scaling * kernel(dual_field)
        return dual_field, marginal_field

    dual_scaling, marginal = lax.map(member_pass, (density, scaling))
    log_marginal = jnp.log(marginal)
    weighted = jnp.einsum("k,kfrc->frc", member_weights, log_marginal, precision=lax.Precision.HIGHEST)
    log_mean = weighted / jnp.sum(member_weights)
    barycenter = jnp.exp(log_mean)
    new_scaling = (scaling * barycenter) / marginal
    return new_scaling, dual_scaling, barycenter
```

```python
import functools

import jax
import jax.numpy as jnp
from jax import lax
from jax.experimental import pallas as pl
from jax.experimental.pallas import tpu as pltpu
from jax.sharding import PartitionSpec as P

STEPS = 4
KAPPA = 0.24
LANES = 128
MESH = pl.DeviceIdType.MESH


def kernel(
    n, members, faces, rows, side,
    seams_ref, weight_ref, density_ref, scaling_ref,
    new_ref, dual_ref, bary_ref,
    field, dens, pack, packs, top, bottom, first, last, above, below,
    table, columns, ghosts, ghost_columns, logs, others,
    pack_send, pack_recv, top_send, bottom_send, row_recv, log_send, log_recv,
):
    t = lax.axis_index("tile")
    m = lax.axis_index("member")
    groups = faces * rows // 8
    per = LANES // 16
    wide = pl.cdiv(groups, per)
    half = LANES // 8
    narrow = pl.cdiv(groups, half)

    barrier = pltpu.get_barrier_semaphore()
    for i in range(1, n):
        pl.semaphore_signal(barrier, inc=1, device_id={"tile": lax.rem(t + i, n)}, device_id_type=MESH)
    for i in range(1, members):
        pl.semaphore_signal(
            barrier, inc=1, device_id={"member": lax.rem(m + i, members)}, device_id_type=MESH
        )

    lane = lax.broadcasted_iota(jnp.int32, (8, LANES), 1)

    def edge_block(ref, k):
        f, r = (8 * k) // rows, (8 * k) % rows
        low = ref[0, f, r : r + 8, :LANES]
        if side == LANES:
            return low
        return jnp.where(lane < LANES // 2, low, ref[0, f, r : r + 8, side - LANES :])

    for vreg in range(wide):
        out = jnp.ones((8, LANES), jnp.float32)
        for k in range(vreg * per, min(groups, (vreg + 1) * per)):
            at = 16 * (k % per)
            moved = pltpu.roll(edge_block(scaling_ref, k), (8 + at) % LANES, 1)
            out = jnp.where((lane >= at) & (lane < at + 16), moved, out)
        pack[vreg] = out
    for vreg in range(narrow):
        out = jnp.ones((8, LANES), jnp.float32)
        for k in range(vreg * half, min(groups, (vreg + 1) * half)):
            at = 8 * (k % half)
            moved = pltpu.roll(edge_block(density_ref, k), (4 + at) % LANES, 1)
            out = jnp.where((lane >= at) & (lane < at + 8), moved, out)
        pack[wide + vreg] = out
    packs[t] = pack[...]
    top[:faces] = scaling_ref[0, :, :8, :]
    bottom[:faces] = scaling_ref[0, :, rows - 8 :, :]
    for f in range(faces):
        j, s = faces + f // 2, 4 * (f % 2)
        top[j, s : s + 4, :] = density_ref[0, f, :4, :]
        bottom[j, s : s + 4, :] = density_ref[0, f, rows - 4 :, :]

    pl.semaphore_wait(barrier, n - 1 + members - 1)

    def send_pack(peer, slot):
        return pltpu.make_async_remote_copy(
            src_ref=pack, dst_ref=packs.at[slot],
            send_sem=pack_send.at[peer], recv_sem=pack_recv.at[slot],
            device_id={"tile": peer}, device_id_type=MESH,
        )

    def send_rows(src, dst, sems, sem, which, peer):
        return pltpu.make_async_remote_copy(
            src_ref=src, dst_ref=dst, send_sem=sems.at[sem], recv_sem=row_recv.at[which],
            device_id={"tile": peer}, device_id_type=MESH,
        )

    peers = [lax.rem(t + i, n) for i in range(1, n)]
    up_peer = lax.rem(t + n - 1, n)
    down_peer = lax.rem(t + 1, n)
    to_above = send_rows(top, below, top_send, n, 3, up_peer)
    to_below = send_rows(bottom, above, bottom_send, n, 2, down_peer)
    to_first = [send_rows(top, first, top_send, i, 0, peer) for i, peer in enumerate(peers)]
    to_last = [send_rows(bottom, last, bottom_send, i, 1, peer) for i, peer in enumerate(peers)]

    @pl.when(t == 0)
    def _():
        for copy in reversed(to_first):
            copy.start()

    @pl.when(t == n - 1)
    def _():
        for copy in to_last:
            copy.start()

    @pl.when(t > 0)
    def _():
        to_above.start()

    @pl.when(t < n - 1)
    def _():
        to_below.start()

    for peer in peers:
        send_pack(peer, t).start()

    def fill(i, carry):
        at = pl.multiple_of(8 * i, 8)
        for f in range(faces):
            block = jnp.ones((8, side), jnp.float32)
            dens[f, pl.ds(at, 8), :] = block
            field[0, f, pl.ds(at + 8, 8), :] = block
        return carry

    lax.fori_loop(0, side // 8, fill, 0)
    ghosts[...] = jnp.zeros(ghosts.shape, jnp.float32)
    table[...] = jnp.zeros(table.shape, jnp.float32)

    for peer in peers:
        send_pack(peer, peer).wait_recv()

    for s in range(n):
        for k in range(groups):
            f, r = (8 * k) // rows, (8 * k) % rows + rows * s
            value = pltpu.roll(packs[s, k // per], (2 * LANES - 8 - 16 * (k % per)) % LANES, 1)
            field[0, f, 8 + r : 16 + r, :LANES] = value
            other = pltpu.roll(packs[s, wide + k // half], (2 * LANES - 4 - 8 * (k % half)) % LANES, 1)
            dens[f, r : r + 8, :LANES] = other
            if side > LANES:
                field[0, f, 8 + r : 16 + r, side - LANES :] = value
                dens[f, r : r + 8, side - LANES :] = other

    start = pl.multiple_of(rows * t, 8)

    def place(src, at, low):
        at = pl.multiple_of(at, 8) if not isinstance(at, int) else at
        field[0, :, pl.ds(at + 8, 8), :] = src[:faces]
        for f in range(faces):
            j, s = faces + f // 2, 4 * (f % 2)
            four = src[j, s : s + 4, :]
            line_of = lax.broadcasted_iota(jnp.int32, (8, side), 0)
            dens[f, pl.ds(at, 8), :] = jnp.where(
                line_of < 4 if low else line_of >= 4,
                jnp.concatenate([four, four], axis=0),
                dens[f, pl.ds(at, 8), :],
            )

    @pl.when(t > 0)
    def _():
        to_first[0].wait_recv()
        place(first, 0, True)

    @pl.when(t < n - 1)
    def _():
        to_last[0].wait_recv()
        place(last, side - 8, False)

    @pl.when(t > 0)
    def _():
        to_below.wait_recv()
        place(above, start - 8, False)

    @pl.when(t < n - 1)
    def _():
        to_above.wait_recv()
        place(below, start + rows, True)

    field[0, :, pl.ds(start + 8, rows), :] = scaling_ref[0]
    dens[:, pl.ds(start, rows), :] = density_ref[0]

    slots = []
    for e in range(4):
        slots.append([])
        for f in range(faces):
            g, edge, flip = seams_ref[0, e, f], seams_ref[1, e, f], seams_ref[2, e, f]
            base = jnp.where(edge < 2, 2 * faces + 2 * g + edge, 2 * g + 3 - edge)
            slots[e].append(base + 32 * jnp.where(flip == 1, 1, 0))

    reverse = LANES - 1 - lane
    blocks = side // LANES

    def diffuse(step, carry):
        now = lax.rem(step, 2)
        later = 1 - now

        def extract(i, carry):
            at = pl.multiple_of(8 * i, 8)
            out = jnp.zeros((8, LANES), jnp.float32)
            for f in range(faces):
                u = field[now, f, pl.ds(at + 8, 8), :LANES]
                if side > LANES:
                    u = jnp.where(
                        lane < LANES // 2, u, field[now, f, pl.ds(at + 8, 8), side - LANES :]
                    )
                moved = pltpu.roll(u, 1 + 2 * f, 1)
                out = jnp.where((lane >= 2 * f) & (lane < 2 * f + 2), moved, out)
            columns[pl.ds(at, 8), :] = out
            return carry

        lax.fori_loop(0, side // 8, extract, 0, unroll=side == LANES)
        for b in range(blocks):
            cut = slice(b * LANES, (b + 1) * LANES)
            turned = columns[cut, :].T
            table[: 2 * faces, cut] = turned[: 2 * faces]
        for f in range(faces):
            table[2 * faces + 2 * f : 2 * faces + 2 * f + 1, :] = field[now, f, 8:9, :]
            table[2 * faces + 2 * f + 1 : 2 * faces + 2 * f + 2, :] = field[
                now, f, side + 7 : side + 8, :
            ]
        for b in range(blocks):
            back = blocks - 1 - b
            for r in range(0, 4 * faces, 8):
                value = table[r : r + 8, b * LANES : (b + 1) * LANES]
                table[32 + r : 40 + r, back * LANES : (back + 1) * LANES] = jnp.take_along_axis(
                    value, reverse, axis=1, mode="promise_in_bounds"
                )
        for f in range(faces):
            field[now, f, 7:8, :] = table[pl.ds(slots[0][f], 1), :]
            field[now, f, side + 8 : side + 9, :] = table[pl.ds(slots[1][f], 1), :]
            left, right = 2 * f, (2 * f + LANES - 1) % LANES
            ghosts[left : left + 1, :] = table[pl.ds(slots[2][f], 1), :]
            ghosts[right : right + 1, :] = table[pl.ds(slots[3][f], 1), :]
        for b in range(blocks):
            cut = slice(b * LANES, (b + 1) * LANES)
            ghost_columns[cut, :] = ghosts[:, cut].T

        lanes = lax.broadcasted_iota(jnp.int32, (8, side), 1)
        line_of = lax.broadcasted_iota(jnp.int32, (8, side), 0)

        def update(i, carry):
            at = pl.multiple_of(8 * i, 8)
            line = ghost_columns[pl.ds(at, 8), :]
            for f in range(faces):
                u = field[now, f, pl.ds(at + 8, 8), :]
                if blocks == 1:
                    up = field[now, f, pl.ds(at + 7, 8), :]
                    down = field[now, f, pl.ds(at + 9, 8), :]
                else:
                    before = field[now, f, pl.ds(at, 8), :]
                    after = field[now, f, pl.ds(at + 16, 8), :]
                    up = jnp.where(line_of == 0, pltpu.roll(before, 1, 0), pltpu.roll(u, 1, 0))
                    down = jnp.where(line_of == 7, pltpu.roll(after, 7, 0), pltpu.roll(u, 7, 0))
                ghost = pltpu.roll(line, (LANES - 2 * f) % LANES, 1)
                if blocks > 1:
                    ghost = jnp.concatenate([ghost] * blocks, axis=1)
                left = jnp.where(lanes == 0, ghost, pltpu.roll(u, 1, 1))
                right = jnp.where(lanes == side - 1, ghost, pltpu.roll(u, side - 1, 1))
                total = (up + down) + (left + right)
                field[later, f, pl.ds(at + 8, 8), :] = u + KAPPA * (total - 4.0 * u)
            return carry

        lax.fori_loop(0, side // 8, update, 0, unroll=side == LANES)
        return carry

    lax.fori_loop(0, STEPS, diffuse, 0)

    def divide(i, carry):
        at = pl.multiple_of(8 * i, 8)
        for f in range(faces):
            field[0, f, pl.ds(at + 8, 8), :] = (
                dens[f, pl.ds(at, 8), :] / field[0, f, pl.ds(at + 8, 8), :]
            )
        return carry

    lax.fori_loop(0, side // 8, divide, 0, unroll=side == LANES)
    dual_ref[0] = field[0, :, pl.ds(start + 8, rows), :]
    lax.fori_loop(0, STEPS, diffuse, 0)

    weight = weight_ref[0]
    marginal = scaling_ref[0] * field[0, :, pl.ds(start + 8, rows), :]
    logs[:faces] = weight * jnp.log(marginal)
    logs[faces] = jnp.full((rows, side), weight, jnp.float32)

    def send_logs(i, peer, slot):
        return pltpu.make_async_remote_copy(
            src_ref=logs, dst_ref=others.at[slot],
            send_sem=log_send.at[i], recv_sem=log_recv.at[slot],
            device_id={"member": peer}, device_id_type=MESH,
        )

    partners = [lax.rem(m + i, members) for i in range(1, members)]
    for i, peer in enumerate(partners):
        send_logs(i, peer, m).start()
    total = logs[...]
    for i, peer in enumerate(partners):
        send_logs(i, peer, peer).wait_recv()
        total = total + others[peer]
    bary = jnp.exp(total[:faces] / total[faces:])
    bary_ref[...] = bary
    new_ref[0] = (scaling_ref[0] * bary) / marginal

    for i, peer in enumerate(partners):
        send_logs(i, peer, m).wait_send()
    for peer in peers:
        send_pack(peer, t).wait_send()

    @pl.when(t == 0)
    def _():
        for copy in to_first:
            copy.wait_send()

    @pl.when(t == n - 1)
    def _():
        for copy in to_last:
            copy.wait_send()

    @pl.when(t > 0)
    def _():
        to_above.wait_send()

    @pl.when(t < n - 1)
    def _():
        to_below.wait_send()


def body(density, scaling, member_weights, seams):
    n = lax.axis_size("tile")
    members = lax.axis_size("member")
    _, faces, rows, side = scaling.shape
    groups = faces * rows // 8
    packed = pl.cdiv(groups, LANES // 16) + pl.cdiv(groups, LANES // 8)
    lines = faces + pl.cdiv(faces, 2)
    vmem = functools.partial(pltpu.VMEM, dtype=jnp.float32)
    dma = lambda count: pltpu.SemaphoreType.DMA((count,))
    smem = pl.BlockSpec(memory_space=pltpu.SMEM)
    whole = pl.BlockSpec(memory_space=pltpu.VMEM)
    return pl.pallas_call(
        functools.partial(kernel, n, members, faces, rows, side),
        out_shape=(
            jax.ShapeDtypeStruct(scaling.shape, jnp.float32),
            jax.ShapeDtypeStruct(scaling.shape, jnp.float32),
            jax.ShapeDtypeStruct(scaling.shape[1:], jnp.float32),
        ),
        in_specs=[smem, smem, whole, whole],
        out_specs=(whole, whole, whole),
        scratch_shapes=[
            vmem((2, faces, side + 16, side)),
            vmem((faces, side, side)),
            vmem((packed, 8, LANES)),
            vmem((n, packed, 8, LANES)),
            vmem((lines, 8, side)),
            vmem((lines, 8, side)),
            vmem((lines, 8, side)),
            vmem((lines, 8, side)),
            vmem((lines, 8, side)),
            vmem((lines, 8, side)),
            vmem((64, side)),
            vmem((side, LANES)),
            vmem((LANES, side)),
            vmem((side, LANES)),
            vmem((faces + 1, rows, side)),
            vmem((members, faces + 1, rows, side)),
            dma(n), dma(n), dma(n + 1), dma(n + 1), dma(4), dma(members), dma(members),
        ],
        compiler_params=pltpu.CompilerParams(
            collective_id=0, has_side_effects=True, vmem_limit_bytes=48 << 20
        ),
    )(seams, member_weights, density, scaling)


def solution(mesh):
    return jax.shard_map(
        body,
        mesh=mesh,
        in_specs=(
            P("member", None, "tile", None),
            P("member", None, "tile", None),
            P("member"),
            P(),
        ),
        out_specs=(
            P("member", None, "tile", None),
            P("member", None, "tile", None),
            P(None, "tile", None),
        ),
        check_vma=False,
    )
```

```python
import functools

import jax
import jax.numpy as jnp
from jax import lax
from jax.experimental import pallas as pl
from jax.experimental.pallas import tpu as pltpu
from jax.sharding import PartitionSpec as P

STEPS = 4
KAPPA = 0.24
LANES = 128
DEPTH = 8
MESH = pl.DeviceIdType.MESH


def kernel(
    n, members, faces, rows, side,
    seams_ref, weight_ref, density_hbm, scaling_hbm,
    new_ref, dual_ref, bary_ref,
    density, scaling, strips, tile, table, ghosts, ghost_columns,
    pack, packs, first, last, above, below,
    pack_d, packs_d, top_d, bottom_d, first_d, last_d, above_d, below_d,
    logs, others, mine, weights,
    local, pack_send, pack_recv, pack_send_d, pack_recv_d,
    top_send, bottom_send, row_recv, top_send_d, bottom_send_d, row_recv_d,
    log_send, log_recv, weight_send, weight_recv,
):
    t = lax.axis_index("tile")
    m = lax.axis_index("member")
    blocks = side // LANES
    per_block = LANES // rows
    pairs = faces // 2

    barrier = pltpu.get_barrier_semaphore()
    for i in range(1, n):
        pl.semaphore_signal(barrier, inc=1, device_id={"tile": lax.rem(t + i, n)}, device_id_type=MESH)
    for i in range(1, members):
        pl.semaphore_signal(
            barrier, inc=1, device_id={"member": lax.rem(m + i, members)}, device_id_type=MESH
        )
    load_scaling = pltpu.make_async_copy(scaling_hbm.at[0], scaling, local.at[0])
    load_density = pltpu.make_async_copy(density_hbm.at[0], density, local.at[1])
    load_scaling.start()
    load_density.start()

    sub8 = lax.broadcasted_iota(jnp.int32, (8, LANES), 0)
    lane8 = lax.broadcasted_iota(jnp.int32, (8, LANES), 1)
    sub = lax.broadcasted_iota(jnp.int32, (8, side), 0)
    lane = lax.broadcasted_iota(jnp.int32, (8, side), 1)

    def turned_columns(src, at):
        flat = src[:, :, at : at + LANES].reshape(faces * rows, LANES)
        rest = jnp.ones((LANES - faces * rows, LANES), jnp.float32)
        return jnp.concatenate([flat, rest], axis=0).T

    load_scaling.wait()
    turned = turned_columns(scaling, 0)
    pack[0] = turned[:8]
    pack[1] = (turned if blocks == 1 else turned_columns(scaling, side - LANES))[LANES - 8 :]
    packs[t] = pack[...]
    mine[...] = jnp.full((8, LANES), weight_ref[0], jnp.float32)

    peers = [lax.rem(t + i, n) for i in range(1, n)]
    partners = [lax.rem(m + i, members) for i in range(1, members)]

    def remote(src, dst, send, recv, peer, axis="tile"):
        return pltpu.make_async_remote_copy(
            src_ref=src, dst_ref=dst, send_sem=send, recv_sem=recv,
            device_id={axis: peer}, device_id_type=MESH,
        )

    def send_pack(i, slot):
        return remote(pack, packs.at[slot], pack_send.at[i], pack_recv.at[slot], peers[i])

    def send_pack_d(i, slot):
        return remote(pack_d, packs_d.at[slot], pack_send_d.at[i], pack_recv_d.at[slot], peers[i])

    def row_sends(top, bottom, first, last, above, below, top_send, bottom_send, recv):
        up_peer, down_peer = lax.rem(t + n - 1, n), lax.rem(t + 1, n)
        return (
            [remote(top, first, top_send.at[i], recv.at[0], p) for i, p in enumerate(peers)],
            [remote(bottom, last, bottom_send.at[i], recv.at[1], p) for i, p in enumerate(peers)],
            remote(top, below, top_send.at[n], recv.at[2], up_peer),
            remote(bottom, above, bottom_send.at[n], recv.at[3], down_peer),
        )

    lines = row_sends(
        scaling.at[:, pl.ds(0, DEPTH), :], scaling.at[:, pl.ds(rows - DEPTH, DEPTH), :],
        first, last, above, below, top_send, bottom_send, row_recv,
    )
    lines_d = row_sends(
        top_d, bottom_d, first_d, last_d, above_d, below_d, top_send_d, bottom_send_d, row_recv_d
    )

    def on_rows(sends, act):
        to_first, to_last, to_above, to_below = sends

        @pl.when(t == 0)
        def _():
            for copy in reversed(to_first):
                act(copy)

        @pl.when(t == n - 1)
        def _():
            for copy in to_last:
                act(copy)

        @pl.when(t > 0)
        def _():
            act(to_above)

        @pl.when(t < n - 1)
        def _():
            act(to_below)

    def receive_rows(sends):
        to_first, to_last, to_above, to_below = sends

        @pl.when(t > 0)
        def _():
            to_first[0].wait_recv()
            to_below.wait_recv()

        @pl.when(t < n - 1)
        def _():
            to_last[0].wait_recv()
            to_above.wait_recv()

    pl.semaphore_wait(barrier, n - 1 + members - 1)

    on_rows(lines, lambda copy: copy.start())
    for i in range(n - 1):
        send_pack(i, t).start()

    load_density.wait()
    turned = turned_columns(density, 0)
    other = turned if blocks == 1 else turned_columns(density, side - LANES)
    pack_d[...] = jnp.where(sub8 < 4, turned[:8], other[LANES - 8 :])
    packs_d[t] = pack_d[...]
    for j in range(pairs):
        top_d[j] = jnp.where(
            sub < 4, density[2 * j, :8, :], pltpu.roll(density[2 * j + 1, :8, :], 4, 0)
        )
        bottom_d[j] = jnp.where(
            sub >= 4, density[2 * j, rows - 8 :, :], pltpu.roll(density[2 * j + 1, rows - 8 :, :], 4, 0)
        )
    on_rows(lines_d, lambda copy: copy.start())
    for i in range(n - 1):
        send_pack_d(i, t).start()

    def send_weight(i, slot):
        return remote(
            mine, weights.at[slot], weight_send.at[i], weight_recv.at[slot], partners[i], "member"
        )

    for i in range(members - 1):
        send_weight(i, m).start()

    @pl.when(t == 0)
    def _():
        first[...] = scaling[:, :DEPTH, :]
        first_d[...] = top_d[...]
        above[...] = jnp.ones(above.shape, jnp.float32)
        above_d[...] = jnp.ones(above_d.shape, jnp.float32)

    @pl.when(t == n - 1)
    def _():
        last[...] = scaling[:, rows - DEPTH :, :]
        last_d[...] = bottom_d[...]
        below[...] = jnp.ones(below.shape, jnp.float32)
        below_d[...] = jnp.ones(below_d.shape, jnp.float32)

    ghosts[...] = jnp.zeros(ghosts.shape, jnp.float32)
    ghost_columns[...] = jnp.zeros(ghost_columns.shape, jnp.float32)
    table[...] = jnp.zeros(table.shape, jnp.float32)

    slots = []
    for f in range(faces):
        for e in range(4):
            flip = jnp.where(seams_ref[2, e, f] == 1, 32, 0)
            slots.append(4 * seams_ref[0, e, f] + seams_ref[1, e, f] + flip)

    def gather_strip(read, f):
        parts = []
        for b in range(blocks):
            out = jnp.ones((8, LANES), jnp.float32)
            for k in range(per_block):
                shift = (rows * (k - f)) % LANES
                piece = read(b * per_block + k)
                piece = pltpu.roll(piece, shift, 1) if shift else piece
                out = jnp.where((lane8 >= rows * k) & (lane8 < rows * (k + 1)), piece, out)
            parts.append(out)
        return parts[0] if blocks == 1 else jnp.concatenate(parts, axis=1)

    for i in range(n - 1):
        send_pack(i, peers[i]).wait_recv()
    for f in range(faces):
        for k in range(2):
            strips[4 * f + 2 + k] = gather_strip(lambda s: packs[s, k], f)
    receive_rows(lines)
    for f in range(faces):
        strips[4 * f] = first[f]
        strips[4 * f + 1] = last[f]
        tile[f, :8] = above[f]
        tile[f, 8 : 8 + rows] = scaling[f]
        tile[f, 8 + rows :] = below[f]

    start = pl.multiple_of(rows * t, 8)
    reverse = LANES - 1 - lane8
    at_top = (sub == 7) & (t == 0)
    at_bottom = (sub == 0) & (t == n - 1)
    height = (rows + 16) // 8

    def place(line, shift):
        line = pltpu.roll(line, (LANES - shift) % LANES, 1)
        return line if blocks == 1 else jnp.concatenate([line] * blocks, axis=1)

    def stencil(u, up, down, ends):
        left = jnp.where(lane == 0, ends, pltpu.roll(u, 1, 1))
        right = jnp.where(lane == side - 1, ends, pltpu.roll(u, side - 1, 1))
        return u + KAPPA * (((up + down) + (left + right)) - 4.0 * u)

    def diffuse(step, carry):
        for i in range(4 * faces):
            row = 0 if i % 2 == 0 else 7
            table[i : i + 1, :] = strips[i, row : row + 1, :]
        for b in range(blocks):
            back = blocks - 1 - b
            for r in range(0, 4 * faces, 8):
                table[32 + r : 40 + r, back * LANES : (back + 1) * LANES] = jnp.take_along_axis(
                    table[r : r + 8, b * LANES : (b + 1) * LANES], reverse, axis=1,
                    mode="promise_in_bounds",
                )
        for f in range(faces):
            for e in range(4):
                row = 4 * f + 3 - e
                ghosts[row : row + 1, :] = table[pl.ds(slots[4 * f + e], 1), :]
        for b in range(blocks):
            cut = slice(b * LANES, (b + 1) * LANES)
            ghost_columns[8 + b * LANES : 8 + (b + 1) * LANES, :] = ghosts[:, cut].T
        low = ghost_columns[8:16, :]
        high = ghost_columns[side : side + 8, :]

        for f in range(faces):
            for e in range(4):
                u = strips[4 * f + e]
                row = 4 * f + 3 - e
                ghost = jnp.broadcast_to(ghosts[row : row + 1, :], (8, side))
                up, down = pltpu.roll(u, 1, 0), pltpu.roll(u, 7, 0)
                if e % 2 == 0:
                    up = jnp.where(sub == 0, ghost, up)
                else:
                    down = jnp.where(sub == 7, ghost, down)
                ends = place(high if e % 2 else low, 4 * f + 1 + (e // 2) * 2)
                strips[4 * f + e] = stencil(u, up, down, ends)

        for f in range(faces):
            u = [tile[f, 8 * j : 8 * j + 8, :] for j in range(height)]
            over = jnp.broadcast_to(ghosts[4 * f + 3 : 4 * f + 4, :], (8, side))
            under = jnp.broadcast_to(ghosts[4 * f + 2 : 4 * f + 3, :], (8, side))
            u[0] = jnp.where(at_top, over, u[0])
            u[-1] = jnp.where(at_bottom, under, u[-1])
            ups = [pltpu.roll(v, 1, 0) for v in u]
            downs = [pltpu.roll(v, 7, 0) for v in u]
            for j in range(height):
                up = jnp.where(sub == 0, ups[j - 1], ups[j]) if j else ups[j]
                down = jnp.where(sub == 7, downs[j + 1], downs[j]) if j < height - 1 else downs[j]
                ends = place(ghost_columns[pl.ds(start + 8 * j, 8), :], 4 * f + 1)
                tile[f, 8 * j : 8 * j + 8, :] = stencil(u[j], up, down, ends)
        return carry

    lax.fori_loop(0, STEPS, diffuse, 0)

    for i in range(n - 1):
        send_pack_d(i, peers[i]).wait_recv()
    receive_rows(lines_d)
    for f in range(faces):
        columns = gather_strip(lambda s: packs_d[s], f)
        turn = (lambda v: v) if f % 2 == 0 else (lambda v: pltpu.roll(v, 4, 0))
        strips[4 * f] = turn(first_d[f // 2]) / strips[4 * f]
        strips[4 * f + 1] = turn(last_d[f // 2]) / strips[4 * f + 1]
        strips[4 * f + 2] = columns / strips[4 * f + 2]
        strips[4 * f + 3] = columns / strips[4 * f + 3]
        tile[f, :8] = turn(above_d[f // 2]) / tile[f, :8]
        dual = density[f] / tile[f, 8 : 8 + rows]
        tile[f, 8 : 8 + rows] = dual
        dual_ref[0, f] = dual
        tile[f, 8 + rows :] = turn(below_d[f // 2]) / tile[f, 8 + rows :]

    lax.fori_loop(0, STEPS, diffuse, 0)

    marginal = scaling[...] * tile[:, 8 : 8 + rows, :]
    logs[...] = weight_ref[0] * jnp.log(marginal)

    def send_logs(i, slot):
        return remote(logs, others.at[slot], log_send.at[i], log_recv.at[slot], partners[i], "member")

    for i in range(members - 1):
        send_logs(i, m).start()
    weight = mine[...]
    for i in range(members - 1):
        send_weight(i, partners[i]).wait_recv()
        weight = weight + weights[partners[i]]
    if blocks > 1:
        weight = jnp.concatenate([weight] * blocks, axis=1)
    total = logs[...]
    for i in range(members - 1):
        send_logs(i, partners[i]).wait_recv()
        total = total + others[partners[i]]
    bary = jnp.exp(total / weight[:1].reshape(1, 1, side))
    bary_ref[...] = bary
    new_ref[0] = (scaling[...] * bary) / marginal

    for i in range(members - 1):
        send_logs(i, m).wait_send()
        send_weight(i, m).wait_send()
    for i in range(n - 1):
        send_pack(i, t).wait_send()
        send_pack_d(i, t).wait_send()
    on_rows(lines, lambda copy: copy.wait_send())
    on_rows(lines_d, lambda copy: copy.wait_send())


def body(density, scaling, member_weights, seams):
    n = lax.axis_size("tile")
    members = lax.axis_size("member")
    _, faces, rows, side = scaling.shape
    vmem = lambda *shape: pltpu.VMEM(shape, jnp.float32)
    dma = lambda count: pltpu.SemaphoreType.DMA((count,))
    smem = pl.BlockSpec(memory_space=pltpu.SMEM)
    whole = pl.BlockSpec(memory_space=pltpu.VMEM)
    hbm = pl.BlockSpec(memory_space=pltpu.HBM)
    return pl.pallas_call(
        functools.partial(kernel, n, members, faces, rows, side),
        out_shape=(
            jax.ShapeDtypeStruct(scaling.shape, jnp.float32),
            jax.ShapeDtypeStruct(scaling.shape, jnp.float32),
            jax.ShapeDtypeStruct(scaling.shape[1:], jnp.float32),
        ),
        in_specs=[smem, smem, hbm, hbm],
        out_specs=(whole, whole, whole),
        scratch_shapes=[
            vmem(faces, rows, side),
            vmem(faces, rows, side),
            vmem(4 * faces, 8, side),
            vmem(faces, rows + 16, side),
            vmem(64, side),
            vmem(LANES, side),
            vmem(side + 16, LANES),
            vmem(2, 8, LANES),
            vmem(n, 2, 8, LANES),
            *[vmem(faces, DEPTH, side)] * 4,
            vmem(8, LANES),
            vmem(n, 8, LANES),
            *[vmem(faces // 2, 8, side)] * 6,
            vmem(faces, rows, side),
            vmem(members, faces, rows, side),
            vmem(8, LANES),
            vmem(members, 8, LANES),
            dma(2), dma(n), dma(n), dma(n), dma(n),
            dma(n + 1), dma(n + 1), dma(4), dma(n + 1), dma(n + 1), dma(4),
            dma(members), dma(members), dma(members), dma(members),
        ],
        compiler_params=pltpu.CompilerParams(
            collective_id=0, has_side_effects=True
        ),
    )(seams, member_weights, density, scaling)


def solution(mesh):
    return jax.shard_map(
        body,
        mesh=mesh,
        in_specs=(
            P("member", None, "tile", None),
            P("member", None, "tile", None),
            P("member"),
            P(),
        ),
        out_specs=(
            P("member", None, "tile", None),
            P("member", None, "tile", None),
            P(None, "tile", None),
        ),
        check_vma=False,
    )
```

```python
import functools

import jax
import jax.numpy as jnp
from jax import lax
from jax.experimental import pallas as pl
from jax.experimental.pallas import tpu as pltpu
from jax.sharding import PartitionSpec as P

STEPS = 4
KAPPA = 0.24
LANES = 128
DEPTH = 8
MESH = pl.DeviceIdType.MESH


def kernel(
    n, members, faces, rows, side,
    seams_ref, weight_ref, density_hbm, scaling_hbm,
    out_hbm,
    density, scaling, strips, tile, ghosts, ghost_columns, results,
    pack, packs, first, last, above, below,
    pack_d, packs_d, top_d, bottom_d, first_d, last_d, above_d, below_d,
    logs, others, mine, weights,
    local, pack_send, pack_recv, pack_send_d, pack_recv_d,
    top_send, bottom_send, row_recv, top_send_d, bottom_send_d, row_recv_d,
    log_send, log_recv, weight_send, weight_recv,
):
    t = lax.axis_index("tile")
    m = lax.axis_index("member")
    blocks = side // LANES
    per_block = LANES // rows
    pairs = faces // 2

    barrier = pltpu.get_barrier_semaphore()
    for i in range(1, n):
        pl.semaphore_signal(barrier, inc=1, device_id={"tile": lax.rem(t + i, n)}, device_id_type=MESH)
    for i in range(1, members):
        pl.semaphore_signal(
            barrier, inc=1, device_id={"member": lax.rem(m + i, members)}, device_id_type=MESH
        )
    load_scaling = pltpu.make_async_copy(scaling_hbm.at[0], scaling, local.at[0])
    load_density = pltpu.make_async_copy(density_hbm.at[0], density, local.at[1])
    load_scaling.start()
    load_density.start()

    sub8 = lax.broadcasted_iota(jnp.int32, (8, LANES), 0)
    lane8 = lax.broadcasted_iota(jnp.int32, (8, LANES), 1)
    sub = lax.broadcasted_iota(jnp.int32, (8, side), 0)
    lane = lax.broadcasted_iota(jnp.int32, (8, side), 1)

    def turned_columns(src, at):
        flat = src[:, :, at : at + LANES].reshape(faces * rows, LANES)
        rest = jnp.ones((LANES - faces * rows, LANES), jnp.float32)
        return jnp.concatenate([flat, rest], axis=0).T

    load_scaling.wait()
    turned = turned_columns(scaling, 0)
    pack[0] = turned[:8]
    pack[1] = (turned if blocks == 1 else turned_columns(scaling, side - LANES))[LANES - 8 :]
    packs[t] = pack[...]
    mine[...] = jnp.full((8, LANES), weight_ref[0], jnp.float32)

    peers = [lax.rem(t + i, n) for i in range(1, n)]
    partners = [lax.rem(m + i, members) for i in range(1, members)]

    def remote(src, dst, send, recv, peer, axis="tile"):
        return pltpu.make_async_remote_copy(
            src_ref=src, dst_ref=dst, send_sem=send, recv_sem=recv,
            device_id={axis: peer}, device_id_type=MESH,
        )

    def send_pack(i, slot):
        return remote(pack, packs.at[slot], pack_send.at[i], pack_recv.at[slot], peers[i])

    def send_pack_d(i, slot):
        return remote(pack_d, packs_d.at[slot], pack_send_d.at[i], pack_recv_d.at[slot], peers[i])

    def row_sends(top, bottom, first, last, above, below, top_send, bottom_send, recv):
        up_peer, down_peer = lax.rem(t + n - 1, n), lax.rem(t + 1, n)
        return (
            [remote(top, first, top_send.at[i], recv.at[0], p) for i, p in enumerate(peers)],
            [remote(bottom, last, bottom_send.at[i], recv.at[1], p) for i, p in enumerate(peers)],
            remote(top, below, top_send.at[n], recv.at[2], up_peer),
            remote(bottom, above, bottom_send.at[n], recv.at[3], down_peer),
        )

    lines = row_sends(
        scaling.at[:, pl.ds(0, DEPTH), :], scaling.at[:, pl.ds(rows - DEPTH, DEPTH), :],
        first, last, above, below, top_send, bottom_send, row_recv,
    )
    lines_d = row_sends(
        top_d, bottom_d, first_d, last_d, above_d, below_d, top_send_d, bottom_send_d, row_recv_d
    )

    def on_rows(sends, act):
        to_first, to_last, to_above, to_below = sends

        @pl.when(t == 0)
        def _():
            for copy in reversed(to_first):
                act(copy)

        @pl.when(t == n - 1)
        def _():
            for copy in to_last:
                act(copy)

        @pl.when(t > 0)
        def _():
            act(to_above)

        @pl.when(t < n - 1)
        def _():
            act(to_below)

    def receive_rows(sends):
        to_first, to_last, to_above, to_below = sends

        @pl.when(t > 0)
        def _():
            to_first[0].wait_recv()
            to_below.wait_recv()

        @pl.when(t < n - 1)
        def _():
            to_last[0].wait_recv()
            to_above.wait_recv()

    pl.semaphore_wait(barrier, n - 1 + members - 1)

    on_rows(lines, lambda copy: copy.start())
    for i in range(n - 1):
        send_pack(i, t).start()

    load_density.wait()
    turned = turned_columns(density, 0)
    other = turned if blocks == 1 else turned_columns(density, side - LANES)
    pack_d[...] = jnp.where(sub8 < 4, turned[:8], other[LANES - 8 :])
    packs_d[t] = pack_d[...]
    for j in range(pairs):
        top_d[j] = jnp.where(
            sub < 4, density[2 * j, :8, :], pltpu.roll(density[2 * j + 1, :8, :], 4, 0)
        )
        bottom_d[j] = jnp.where(
            sub >= 4, density[2 * j, rows - 8 :, :], pltpu.roll(density[2 * j + 1, rows - 8 :, :], 4, 0)
        )
    on_rows(lines_d, lambda copy: copy.start())
    for i in range(n - 1):
        send_pack_d(i, t).start()

    def send_weight(i, slot):
        return remote(
            mine, weights.at[slot], weight_send.at[i], weight_recv.at[slot], partners[i], "member"
        )

    for i in range(members - 1):
        send_weight(i, m).start()

    @pl.when(t == 0)
    def _():
        first[...] = scaling[:, :DEPTH, :]
        first_d[...] = top_d[...]
        above[...] = jnp.ones(above.shape, jnp.float32)
        above_d[...] = jnp.ones(above_d.shape, jnp.float32)

    @pl.when(t == n - 1)
    def _():
        last[...] = scaling[:, rows - DEPTH :, :]
        last_d[...] = bottom_d[...]
        below[...] = jnp.ones(below.shape, jnp.float32)
        below_d[...] = jnp.ones(below_d.shape, jnp.float32)

    ghosts[...] = jnp.zeros(ghosts.shape, jnp.float32)
    ghost_columns[...] = jnp.zeros(ghost_columns.shape, jnp.float32)

    where_from = {}
    row_of = lax.broadcasted_iota(jnp.int32, (32, LANES), 0)
    flipped = jnp.zeros((32, LANES), jnp.int32)
    for f in range(faces):
        for e in range(4):
            edge = seams_ref[1, e, f]
            where_from[f, e] = (4 * seams_ref[0, e, f] + edge, 7 * lax.rem(edge, 2))
            flipped = jnp.where(row_of == 4 * f + 3 - e, seams_ref[2, e, f], flipped)
    turns = flipped == 1

    def gather_strip(read, f):
        parts = []
        for b in range(blocks):
            out = jnp.ones((8, LANES), jnp.float32)
            for k in range(per_block):
                shift = (rows * (k - f)) % LANES
                piece = read(b * per_block + k)
                piece = pltpu.roll(piece, shift, 1) if shift else piece
                out = jnp.where((lane8 >= rows * k) & (lane8 < rows * (k + 1)), piece, out)
            parts.append(out)
        return parts[0] if blocks == 1 else jnp.concatenate(parts, axis=1)

    for i in range(n - 1):
        send_pack(i, peers[i]).wait_recv()
    for f in range(faces):
        for k in range(2):
            strips[4 * f + 2 + k] = gather_strip(lambda s: packs[s, k], f)
    receive_rows(lines)
    for f in range(faces):
        strips[4 * f] = first[f]
        strips[4 * f + 1] = last[f]
        tile[f, :8] = above[f]
        tile[f, 8 : 8 + rows] = scaling[f]
        tile[f, 8 + rows :] = below[f]

    start = pl.multiple_of(rows * t, 8)
    reverse = LANES - 1 - lane8
    at_top = (sub == 7) & (t == 0)
    at_bottom = (sub == 0) & (t == n - 1)
    height = (rows + 16) // 8

    def place(line, shift):
        line = pltpu.roll(line, (LANES - shift) % LANES, 1)
        return line if blocks == 1 else jnp.concatenate([line] * blocks, axis=1)

    def stencil(u, up, down, ends):
        left = jnp.where(lane == 0, ends, pltpu.roll(u, 1, 1))
        right = jnp.where(lane == side - 1, ends, pltpu.roll(u, side - 1, 1))
        return u + KAPPA * (((up + down) + (left + right)) - 4.0 * u)

    def diffuse(step, carry):
        for f in range(faces):
            for e in range(4):
                row = 4 * f + 3 - e
                strip, line = where_from[f, e]
                ghosts[row : row + 1, :] = strips[strip, pl.ds(line, 1), :]
        lines = [ghosts[:, b * LANES : (b + 1) * LANES] for b in range(blocks)]
        for b in range(blocks):
            backward = jnp.concatenate(
                [
                    jnp.take_along_axis(
                        lines[blocks - 1 - b][r : r + 8], reverse, axis=1, mode="promise_in_bounds"
                    )
                    for r in range(0, 32, 8)
                ],
                axis=0,
            )
            line = jnp.where(turns, backward, lines[b])
            ghosts[:, b * LANES : (b + 1) * LANES] = line
            ghost_columns[8 + b * LANES : 8 + (b + 1) * LANES, :32] = line.T
        low = ghost_columns[8:16, :]
        high = ghost_columns[side : side + 8, :]

        for f in range(faces):
            for e in range(4):
                u = strips[4 * f + e]
                row = 4 * f + 3 - e
                ghost = jnp.broadcast_to(ghosts[row : row + 1, :], (8, side))
                up, down = pltpu.roll(u, 1, 0), pltpu.roll(u, 7, 0)
                if e % 2 == 0:
                    up = jnp.where(sub == 0, ghost, up)
                else:
                    down = jnp.where(sub == 7, ghost, down)
                ends = place(high if e % 2 else low, 4 * f + 1 + (e // 2) * 2)
                strips[4 * f + e] = stencil(u, up, down, ends)

        for f in range(faces):
            u = [tile[f, 8 * j : 8 * j + 8, :] for j in range(height)]
            over = jnp.broadcast_to(ghosts[4 * f + 3 : 4 * f + 4, :], (8, side))
            under = jnp.broadcast_to(ghosts[4 * f + 2 : 4 * f + 3, :], (8, side))
            u[0] = jnp.where(at_top, over, u[0])
            u[-1] = jnp.where(at_bottom, under, u[-1])
            ups = [pltpu.roll(v, 1, 0) for v in u]
            downs = [pltpu.roll(v, 7, 0) for v in u]
            for j in range(height):
                up = jnp.where(sub == 0, ups[j - 1], ups[j]) if j else ups[j]
                down = jnp.where(sub == 7, downs[j + 1], downs[j]) if j < height - 1 else downs[j]
                ends = place(ghost_columns[pl.ds(start + 8 * j, 8), :], 4 * f + 1)
                tile[f, 8 * j : 8 * j + 8, :] = stencil(u[j], up, down, ends)
        return carry

    lax.fori_loop(0, STEPS, diffuse, 0)

    for i in range(n - 1):
        send_pack_d(i, peers[i]).wait_recv()
    receive_rows(lines_d)
    for f in range(faces):
        columns = gather_strip(lambda s: packs_d[s], f)
        turn = (lambda v: v) if f % 2 == 0 else (lambda v: pltpu.roll(v, 4, 0))
        strips[4 * f] = turn(first_d[f // 2]) / strips[4 * f]
        strips[4 * f + 1] = turn(last_d[f // 2]) / strips[4 * f + 1]
        strips[4 * f + 2] = columns / strips[4 * f + 2]
        strips[4 * f + 3] = columns / strips[4 * f + 3]
        tile[f, :8] = turn(above_d[f // 2]) / tile[f, :8]
        dual = density[f] / tile[f, 8 : 8 + rows]
        tile[f, 8 : 8 + rows] = dual
        results[1, f] = dual
        tile[f, 8 + rows :] = turn(below_d[f // 2]) / tile[f, 8 + rows :]

    store_dual = pltpu.make_async_copy(results.at[1], out_hbm.at[1], local.at[2])
    store_dual.start()
    lax.fori_loop(0, STEPS, diffuse, 0)

    marginal = scaling[...] * tile[:, 8 : 8 + rows, :]
    logs[...] = weight_ref[0] * jnp.log(marginal)

    def send_logs(i, slot):
        return remote(logs, others.at[slot], log_send.at[i], log_recv.at[slot], partners[i], "member")

    for i in range(members - 1):
        send_logs(i, m).start()
    weight = mine[...]
    for i in range(members - 1):
        send_weight(i, partners[i]).wait_recv()
        weight = weight + weights[partners[i]]
    if blocks > 1:
        weight = jnp.concatenate([weight] * blocks, axis=1)
    total = logs[...]
    for i in range(members - 1):
        send_logs(i, partners[i]).wait_recv()
        total = total + others[partners[i]]
    bary = jnp.exp(total / weight[:1].reshape(1, 1, side))
    results[2] = bary
    store_bary = pltpu.make_async_copy(results.at[2], out_hbm.at[2], local.at[1])
    store_bary.start()
    results[0] = (scaling[...] * bary) / marginal
    store_new = pltpu.make_async_copy(results.at[0], out_hbm.at[0], local.at[0])
    store_new.start()

    for i in range(members - 1):
        send_logs(i, m).wait_send()
        send_weight(i, m).wait_send()
    for i in range(n - 1):
        send_pack(i, t).wait_send()
        send_pack_d(i, t).wait_send()
    on_rows(lines, lambda copy: copy.wait_send())
    on_rows(lines_d, lambda copy: copy.wait_send())
    store_dual.wait()
    store_bary.wait()
    store_new.wait()


def hand_out(results, new_hbm, dual_hbm, bary_hbm, sems):
    copies = [
        pltpu.make_async_copy(results.at[0], new_hbm.at[0], sems.at[0]),
        pltpu.make_async_copy(results.at[1], dual_hbm.at[0], sems.at[1]),
        pltpu.make_async_copy(results.at[2], bary_hbm, sems.at[2]),
    ]
    for copy in copies:
        copy.start()
    for copy in copies:
        copy.wait()


def body(density, scaling, member_weights, seams):
    n = lax.axis_size("tile")
    members = lax.axis_size("member")
    _, faces, rows, side = scaling.shape
    vmem = lambda *shape: pltpu.VMEM(shape, jnp.float32)
    dma = lambda count: pltpu.SemaphoreType.DMA((count,))
    smem = pl.BlockSpec(memory_space=pltpu.SMEM)
    hbm = pl.BlockSpec(memory_space=pltpu.HBM)
    results = pl.pallas_call(
        functools.partial(kernel, n, members, faces, rows, side),
        out_shape=jax.ShapeDtypeStruct((3, faces, rows, side), jnp.float32),
        in_specs=[smem, smem, hbm, hbm],
        out_specs=hbm,
        scratch_shapes=[
            vmem(faces, rows, side),
            vmem(faces, rows, side),
            vmem(4 * faces, 8, side),
            vmem(faces, rows + 16, side),
            vmem(32, side),
            vmem(side + 16, LANES),
            vmem(3, faces, rows, side),
            vmem(2, 8, LANES),
            vmem(n, 2, 8, LANES),
            *[vmem(faces, DEPTH, side)] * 4,
            vmem(8, LANES),
            vmem(n, 8, LANES),
            *[vmem(faces // 2, 8, side)] * 6,
            vmem(faces, rows, side),
            vmem(members, faces, rows, side),
            vmem(8, LANES),
            vmem(members, 8, LANES),
            dma(3), dma(n), dma(n), dma(n), dma(n),
            dma(n + 1), dma(n + 1), dma(4), dma(n + 1), dma(n + 1), dma(4),
            dma(members), dma(members), dma(members), dma(members),
        ],
        compiler_params=pltpu.CompilerParams(
            collective_id=0, has_side_effects=True
        ),
    )(seams, member_weights, density, scaling)
    return pl.pallas_call(
        hand_out,
        out_shape=(
            jax.ShapeDtypeStruct(scaling.shape, jnp.float32),
            jax.ShapeDtypeStruct(scaling.shape, jnp.float32),
            jax.ShapeDtypeStruct(scaling.shape[1:], jnp.float32),
        ),
        in_specs=[hbm],
        out_specs=(hbm, hbm, hbm),
        scratch_shapes=[dma(3)],
    )(results)


def solution(mesh):
    return jax.shard_map(
        body,
        mesh=mesh,
        in_specs=(
            P("member", None, "tile", None),
            P("member", None, "tile", None),
            P("member"),
            P(),
        ),
        out_specs=(
            P("member", None, "tile", None),
            P("member", None, "tile", None),
            P(None, "tile", None),
        ),
        check_vma=False,
    )
```

```python
import functools

import jax
import jax.numpy as jnp
from jax import lax
from jax.experimental import pallas as pl
from jax.experimental.pallas import tpu as pltpu
from jax.sharding import PartitionSpec as P

STEPS = 4
KAPPA = 0.24
LANES = 128
DEPTH = 8
MESH = pl.DeviceIdType.MESH


def kernel(
    n, members, faces, rows, side,
    seams_ref, weight_ref, density_hbm, scaling_hbm,
    out_hbm,
    density, scaling, strips, tile, ghosts, ghost_columns, results,
    pack, packs, first, last, above, below,
    pack_d, packs_d, top_d, bottom_d, first_d, last_d, above_d, below_d,
    logs, others, mine, weights,
    local, pack_send, pack_recv, pack_send_d, pack_recv_d,
    top_send, bottom_send, row_recv, top_send_d, bottom_send_d, row_recv_d,
    log_send, log_recv, weight_send, weight_recv,
):
    t = lax.axis_index("tile")
    m = lax.axis_index("member")
    blocks = side // LANES
    per_block = LANES // rows
    pairs = faces // 2

    packs[...] = jnp.ones(packs.shape, jnp.float32)
    packs_d[...] = jnp.ones(packs_d.shape, jnp.float32)

    barrier = pltpu.get_barrier_semaphore()
    for i in range(1, n):
        pl.semaphore_signal(barrier, inc=1, device_id={"tile": lax.rem(t + i, n)}, device_id_type=MESH)
    for i in range(1, members):
        pl.semaphore_signal(
            barrier, inc=1, device_id={"member": lax.rem(m + i, members)}, device_id_type=MESH
        )
    load_scaling = pltpu.make_async_copy(scaling_hbm.at[0], scaling, local.at[0])
    load_density = pltpu.make_async_copy(density_hbm.at[0], density, local.at[1])
    load_scaling.start()
    load_density.start()

    sub8 = lax.broadcasted_iota(jnp.int32, (8, LANES), 0)
    lane8 = lax.broadcasted_iota(jnp.int32, (8, LANES), 1)
    sub = lax.broadcasted_iota(jnp.int32, (8, side), 0)
    lane = lax.broadcasted_iota(jnp.int32, (8, side), 1)

    def turned_columns(src, at):
        flat = src[:, :, at : at + LANES].reshape(faces * rows, LANES)
        rest = jnp.ones((LANES - faces * rows, LANES), jnp.float32)
        return jnp.concatenate([flat, rest], axis=0).T

    load_scaling.wait()
    turned = turned_columns(scaling, 0)
    pack[0] = turned[:8]
    pack[1] = (turned if blocks == 1 else turned_columns(scaling, side - LANES))[LANES - 8 :]
    packs[t] = pack[...]
    mine[...] = jnp.full((8, LANES), weight_ref[0], jnp.float32)

    peers = [lax.rem(t + i, n) for i in range(1, n)]
    partners = [lax.rem(m + i, members) for i in range(1, members)]

    def remote(src, dst, send, recv, peer, axis="tile"):
        return pltpu.make_async_remote_copy(
            src_ref=src, dst_ref=dst, send_sem=send, recv_sem=recv,
            device_id={axis: peer}, device_id_type=MESH,
        )

    def send_pack(i, slot):
        return remote(pack, packs.at[slot], pack_send.at[i], pack_recv.at[slot], peers[i])

    def send_pack_d(i, slot):
        return remote(pack_d, packs_d.at[slot], pack_send_d.at[i], pack_recv_d.at[slot], peers[i])

    def reaches(source, target):
        mirror = n - 1 - target
        ends = (target == 0) | (target == n - 1)
        return ends | (jnp.abs(source - target) <= 1) | (jnp.abs(source - mirror) <= 1)

    def on_packs(sends, act, arriving):
        for i in range(n - 1):

            @pl.when(reaches(peers[i], t) if arriving else reaches(t, peers[i]))
            def _():
                act(sends(i, peers[i] if arriving else t))

    def row_sends(top, bottom, first, last, above, below, top_send, bottom_send, recv):
        up_peer, down_peer = lax.rem(t + n - 1, n), lax.rem(t + 1, n)
        return (
            [remote(top, first, top_send.at[i], recv.at[0], p) for i, p in enumerate(peers)],
            [remote(bottom, last, bottom_send.at[i], recv.at[1], p) for i, p in enumerate(peers)],
            remote(top, below, top_send.at[n], recv.at[2], up_peer),
            remote(bottom, above, bottom_send.at[n], recv.at[3], down_peer),
        )

    lines = row_sends(
        scaling.at[:, pl.ds(0, DEPTH), :], scaling.at[:, pl.ds(rows - DEPTH, DEPTH), :],
        first, last, above, below, top_send, bottom_send, row_recv,
    )
    lines_d = row_sends(
        top_d, bottom_d, first_d, last_d, above_d, below_d, top_send_d, bottom_send_d, row_recv_d
    )

    def on_rows(sends, act):
        to_first, to_last, to_above, to_below = sends

        @pl.when(t == 0)
        def _():
            for copy in reversed(to_first):
                act(copy)

        @pl.when(t == n - 1)
        def _():
            for copy in to_last:
                act(copy)

        @pl.when(t > 0)
        def _():
            act(to_above)

        @pl.when(t < n - 1)
        def _():
            act(to_below)

    def receive_rows(sends):
        to_first, to_last, to_above, to_below = sends

        @pl.when(t > 0)
        def _():
            to_first[0].wait_recv()
            to_below.wait_recv()

        @pl.when(t < n - 1)
        def _():
            to_last[0].wait_recv()
            to_above.wait_recv()

    pl.semaphore_wait(barrier, n - 1 + members - 1)

    on_packs(send_pack, lambda copy: copy.start(), False)
    on_rows(lines, lambda copy: copy.start())

    load_density.wait()
    turned = turned_columns(density, 0)
    other = turned if blocks == 1 else turned_columns(density, side - LANES)
    pack_d[...] = jnp.where(sub8 < 4, turned[:8], other[LANES - 8 :])
    packs_d[t] = pack_d[...]
    for j in range(pairs):
        top_d[j] = jnp.where(
            sub < 4, density[2 * j, :8, :], pltpu.roll(density[2 * j + 1, :8, :], 4, 0)
        )
        bottom_d[j] = jnp.where(
            sub >= 4, density[2 * j, rows - 8 :, :], pltpu.roll(density[2 * j + 1, rows - 8 :, :], 4, 0)
        )
    on_packs(send_pack_d, lambda copy: copy.start(), False)
    on_rows(lines_d, lambda copy: copy.start())

    def send_weight(i, slot):
        return remote(
            mine, weights.at[slot], weight_send.at[i], weight_recv.at[slot], partners[i], "member"
        )

    for i in range(members - 1):
        send_weight(i, m).start()

    @pl.when(t == 0)
    def _():
        first[...] = scaling[:, :DEPTH, :]
        first_d[...] = top_d[...]
        above[...] = jnp.ones(above.shape, jnp.float32)
        above_d[...] = jnp.ones(above_d.shape, jnp.float32)

    @pl.when(t == n - 1)
    def _():
        last[...] = scaling[:, rows - DEPTH :, :]
        last_d[...] = bottom_d[...]
        below[...] = jnp.ones(below.shape, jnp.float32)
        below_d[...] = jnp.ones(below_d.shape, jnp.float32)

    ghosts[...] = jnp.zeros(ghosts.shape, jnp.float32)
    ghost_columns[...] = jnp.zeros(ghost_columns.shape, jnp.float32)

    where_from = {}
    row_of = lax.broadcasted_iota(jnp.int32, (32, LANES), 0)
    flipped = jnp.zeros((32, LANES), jnp.int32)
    for f in range(faces):
        for e in range(4):
            edge = seams_ref[1, e, f]
            where_from[f, e] = (4 * seams_ref[0, e, f] + edge, 7 * lax.rem(edge, 2))
            flipped = jnp.where(row_of == 4 * f + 3 - e, seams_ref[2, e, f], flipped)
    turns = flipped == 1

    def gather_strip(read, f):
        parts = []
        for b in range(blocks):
            out = jnp.ones((8, LANES), jnp.float32)
            for k in range(per_block):
                shift = (rows * (k - f)) % LANES
                piece = read(b * per_block + k)
                piece = pltpu.roll(piece, shift, 1) if shift else piece
                out = jnp.where((lane8 >= rows * k) & (lane8 < rows * (k + 1)), piece, out)
            parts.append(out)
        return parts[0] if blocks == 1 else jnp.concatenate(parts, axis=1)

    on_packs(send_pack, lambda copy: copy.wait_recv(), True)
    for f in range(faces):
        for k in range(2):
            strips[4 * f + 2 + k] = gather_strip(lambda s: packs[s, k], f)
    receive_rows(lines)
    for f in range(faces):
        strips[4 * f] = first[f]
        strips[4 * f + 1] = last[f]
        tile[f, :8] = above[f]
        tile[f, 8 : 8 + rows] = scaling[f]
        tile[f, 8 + rows :] = below[f]

    start = pl.multiple_of(rows * t, 8)
    reverse = LANES - 1 - lane8
    at_top = (sub == 7) & (t == 0)
    at_bottom = (sub == 0) & (t == n - 1)
    height = (rows + 16) // 8

    def place(line, shift):
        line = pltpu.roll(line, (LANES - shift) % LANES, 1)
        return line if blocks == 1 else jnp.concatenate([line] * blocks, axis=1)

    def stencil(u, up, down, ends):
        left = jnp.where(lane == 0, ends, pltpu.roll(u, 1, 1))
        right = jnp.where(lane == side - 1, ends, pltpu.roll(u, side - 1, 1))
        return u + KAPPA * (((up + down) + (left + right)) - 4.0 * u)

    def diffuse(step, carry):
        for f in range(faces):
            for e in range(4):
                row = 4 * f + 3 - e
                strip, line = where_from[f, e]
                ghosts[row : row + 1, :] = strips[strip, pl.ds(line, 1), :]
        lines = [ghosts[:, b * LANES : (b + 1) * LANES] for b in range(blocks)]
        for b in range(blocks):
            backward = jnp.concatenate(
                [
                    jnp.take_along_axis(
                        lines[blocks - 1 - b][r : r + 8], reverse, axis=1, mode="promise_in_bounds"
                    )
                    for r in range(0, 32, 8)
                ],
                axis=0,
            )
            line = jnp.where(turns, backward, lines[b])
            ghosts[:, b * LANES : (b + 1) * LANES] = line
            ghost_columns[8 + b * LANES : 8 + (b + 1) * LANES, :32] = line.T
        low = ghost_columns[8:16, :]
        high = ghost_columns[side : side + 8, :]

        for f in range(faces):
            for e in range(4):
                u = strips[4 * f + e]
                row = 4 * f + 3 - e
                ghost = jnp.broadcast_to(ghosts[row : row + 1, :], (8, side))
                up, down = pltpu.roll(u, 1, 0), pltpu.roll(u, 7, 0)
                if e % 2 == 0:
                    up = jnp.where(sub == 0, ghost, up)
                else:
                    down = jnp.where(sub == 7, ghost, down)
                ends = place(high if e % 2 else low, 4 * f + 1 + (e // 2) * 2)
                strips[4 * f + e] = stencil(u, up, down, ends)

        for f in range(faces):
            u = [tile[f, 8 * j : 8 * j + 8, :] for j in range(height)]
            over = jnp.broadcast_to(ghosts[4 * f + 3 : 4 * f + 4, :], (8, side))
            under = jnp.broadcast_to(ghosts[4 * f + 2 : 4 * f + 3, :], (8, side))
            u[0] = jnp.where(at_top, over, u[0])
            u[-1] = jnp.where(at_bottom, under, u[-1])
            ups = [pltpu.roll(v, 1, 0) for v in u]
            downs = [pltpu.roll(v, 7, 0) for v in u]
            for j in range(height):
                up = jnp.where(sub == 0, ups[j - 1], ups[j]) if j else ups[j]
                down = jnp.where(sub == 7, downs[j + 1], downs[j]) if j < height - 1 else downs[j]
                ends = place(ghost_columns[pl.ds(start + 8 * j, 8), :], 4 * f + 1)
                tile[f, 8 * j : 8 * j + 8, :] = stencil(u[j], up, down, ends)
        return carry

    lax.fori_loop(0, STEPS, diffuse, 0)

    on_packs(send_pack_d, lambda copy: copy.wait_recv(), True)
    receive_rows(lines_d)
    for f in range(faces):
        columns = gather_strip(lambda s: packs_d[s], f)
        turn = (lambda v: v) if f % 2 == 0 else (lambda v: pltpu.roll(v, 4, 0))
        strips[4 * f] = turn(first_d[f // 2]) / strips[4 * f]
        strips[4 * f + 1] = turn(last_d[f // 2]) / strips[4 * f + 1]
        strips[4 * f + 2] = columns / strips[4 * f + 2]
        strips[4 * f + 3] = columns / strips[4 * f + 3]
        tile[f, :8] = turn(above_d[f // 2]) / tile[f, :8]
        dual = density[f] / tile[f, 8 : 8 + rows]
        tile[f, 8 : 8 + rows] = dual
        results[1, f] = dual
        tile[f, 8 + rows :] = turn(below_d[f // 2]) / tile[f, 8 + rows :]

    store_dual = pltpu.make_async_copy(results.at[1], out_hbm.at[1], local.at[2])
    store_dual.start()
    lax.fori_loop(0, STEPS, diffuse, 0)

    marginal = scaling[...] * tile[:, 8 : 8 + rows, :]
    logs[...] = weight_ref[0] * jnp.log(marginal)

    def send_logs(i, slot):
        return remote(logs, others.at[slot], log_send.at[i], log_recv.at[slot], partners[i], "member")

    for i in range(members - 1):
        send_logs(i, m).start()
    weight = mine[...]
    for i in range(members - 1):
        send_weight(i, partners[i]).wait_recv()
        weight = weight + weights[partners[i]]
    if blocks > 1:
        weight = jnp.concatenate([weight] * blocks, axis=1)
    total = logs[...]
    for i in range(members - 1):
        send_logs(i, partners[i]).wait_recv()
        total = total + others[partners[i]]
    bary = jnp.exp(total / weight[:1].reshape(1, 1, side))
    results[2] = bary
    store_bary = pltpu.make_async_copy(results.at[2], out_hbm.at[2], local.at[1])
    store_bary.start()
    results[0] = (scaling[...] * bary) / marginal
    store_new = pltpu.make_async_copy(results.at[0], out_hbm.at[0], local.at[0])
    store_new.start()

    for i in range(members - 1):
        send_logs(i, m).wait_send()
        send_weight(i, m).wait_send()
    on_packs(send_pack, lambda copy: copy.wait_send(), False)
    on_packs(send_pack_d, lambda copy: copy.wait_send(), False)
    on_rows(lines, lambda copy: copy.wait_send())
    on_rows(lines_d, lambda copy: copy.wait_send())
    store_dual.wait()
    store_bary.wait()
    store_new.wait()


def hand_out(results, new_hbm, dual_hbm, bary_hbm, held, loaded, stored):
    targets = (new_hbm.at[0], dual_hbm.at[0], bary_hbm)
    loads = [pltpu.make_async_copy(results.at[i], held.at[i], loaded.at[i]) for i in range(3)]
    stores = [pltpu.make_async_copy(held.at[i], targets[i], stored.at[i]) for i in range(3)]
    for load in loads:
        load.start()
    for load, store in zip(loads, stores):
        load.wait()
        store.start()
    for store in stores:
        store.wait()


def body(density, scaling, member_weights, seams):
    n = lax.axis_size("tile")
    members = lax.axis_size("member")
    _, faces, rows, side = scaling.shape
    vmem = lambda *shape: pltpu.VMEM(shape, jnp.float32)
    dma = lambda count: pltpu.SemaphoreType.DMA((count,))
    smem = pl.BlockSpec(memory_space=pltpu.SMEM)
    hbm = pl.BlockSpec(memory_space=pltpu.HBM)
    results = pl.pallas_call(
        functools.partial(kernel, n, members, faces, rows, side),
        out_shape=jax.ShapeDtypeStruct((3, faces, rows, side), jnp.float32),
        in_specs=[smem, smem, hbm, hbm],
        out_specs=hbm,
        scratch_shapes=[
            vmem(faces, rows, side),
            vmem(faces, rows, side),
            vmem(4 * faces, 8, side),
            vmem(faces, rows + 16, side),
            vmem(32, side),
            vmem(side + 16, LANES),
            vmem(3, faces, rows, side),
            vmem(2, 8, LANES),
            vmem(n, 2, 8, LANES),
            *[vmem(faces, DEPTH, side)] * 4,
            vmem(8, LANES),
            vmem(n, 8, LANES),
            *[vmem(faces // 2, 8, side)] * 6,
            vmem(faces, rows, side),
            vmem(members, faces, rows, side),
            vmem(8, LANES),
            vmem(members, 8, LANES),
            dma(3), dma(n), dma(n), dma(n), dma(n),
            dma(n + 1), dma(n + 1), dma(4), dma(n + 1), dma(n + 1), dma(4),
            dma(members), dma(members), dma(members), dma(members),
        ],
        compiler_params=pltpu.CompilerParams(
            collective_id=0, has_side_effects=True
        ),
    )(seams, member_weights, density, scaling)
    return pl.pallas_call(
        hand_out,
        out_shape=(
            jax.ShapeDtypeStruct(scaling.shape, jnp.float32),
            jax.ShapeDtypeStruct(scaling.shape, jnp.float32),
            jax.ShapeDtypeStruct(scaling.shape[1:], jnp.float32),
        ),
        in_specs=[hbm],
        out_specs=(hbm, hbm, hbm),
        scratch_shapes=[vmem(3, faces, rows, side), dma(3), dma(3)],
    )(results)


def solution(mesh):
    return jax.shard_map(
        body,
        mesh=mesh,
        in_specs=(
            P("member", None, "tile", None),
            P("member", None, "tile", None),
            P("member"),
            P(),
        ),
        out_specs=(
            P("member", None, "tile", None),
            P("member", None, "tile", None),
            P(None, "tile", None),
        ),
        check_vma=False,
    )
```

```python
import functools

import jax
import jax.numpy as jnp
from jax import lax
from jax.experimental import pallas as pl
from jax.experimental.pallas import tpu as pltpu
from jax.sharding import PartitionSpec as P

STEPS = 4
KAPPA = 0.24
LANES = 128
DEPTH = 8
MESH = pl.DeviceIdType.MESH


def kernel(
    n, members, faces, rows, side,
    seams_ref, weight_ref, density_hbm, scaling_hbm,
    out_hbm,
    density, scaling, strips, tile, ghosts, ghost_columns, results,
    pack, packs, first, last, above, below,
    pack_d, packs_d, top_d, bottom_d, first_d, last_d, above_d, below_d,
    logs, others, mine, weights,
    local, pack_send, pack_recv, pack_send_d, pack_recv_d,
    top_send, bottom_send, row_recv, top_send_d, bottom_send_d, row_recv_d,
    log_send, log_recv, weight_send, weight_recv,
):
    t = lax.axis_index("tile")
    m = lax.axis_index("member")
    blocks = side // LANES
    per_block = LANES // rows
    pairs = faces // 2

    packs[...] = jnp.ones(packs.shape, jnp.float32)
    packs_d[...] = jnp.ones(packs_d.shape, jnp.float32)

    barrier = pltpu.get_barrier_semaphore()
    for i in range(1, n):
        pl.semaphore_signal(barrier, inc=1, device_id={"tile": lax.rem(t + i, n)}, device_id_type=MESH)
    for i in range(1, members):
        pl.semaphore_signal(
            barrier, inc=1, device_id={"member": lax.rem(m + i, members)}, device_id_type=MESH
        )
    load_scaling = pltpu.make_async_copy(scaling_hbm.at[0], scaling, local.at[0])
    load_density = pltpu.make_async_copy(density_hbm.at[0], density, local.at[1])
    load_scaling.start()
    load_density.start()

    sub8 = lax.broadcasted_iota(jnp.int32, (8, LANES), 0)
    lane8 = lax.broadcasted_iota(jnp.int32, (8, LANES), 1)
    sub = lax.broadcasted_iota(jnp.int32, (8, side), 0)
    lane = lax.broadcasted_iota(jnp.int32, (8, side), 1)

    def turned_columns(src, at):
        flat = src[:, :, at : at + LANES].reshape(faces * rows, LANES)
        rest = jnp.ones((LANES - faces * rows, LANES), jnp.float32)
        return jnp.concatenate([flat, rest], axis=0).T

    load_scaling.wait()
    turned = turned_columns(scaling, 0)
    pack[0] = turned[:8]
    pack[1] = (turned if blocks == 1 else turned_columns(scaling, side - LANES))[LANES - 8 :]
    packs[t] = pack[...]
    mine[...] = jnp.full((8, LANES), weight_ref[0], jnp.float32)

    peers = [lax.rem(t + i, n) for i in range(1, n)]
    partners = [lax.rem(m + i, members) for i in range(1, members)]

    def remote(src, dst, send, recv, peer, axis="tile"):
        return pltpu.make_async_remote_copy(
            src_ref=src, dst_ref=dst, send_sem=send, recv_sem=recv,
            device_id={axis: peer}, device_id_type=MESH,
        )

    def send_pack(i, slot):
        return remote(pack, packs.at[slot], pack_send.at[i], pack_recv.at[slot], peers[i])

    def send_pack_d(i, slot):
        return remote(pack_d, packs_d.at[slot], pack_send_d.at[i], pack_recv_d.at[slot], peers[i])

    def reaches(source, target):
        mirror = n - 1 - target
        ends = (target == 0) | (target == n - 1)
        return ends | (jnp.abs(source - target) <= 1) | (jnp.abs(source - mirror) <= 1)

    def on_packs(sends, act, arriving):
        for i in range(n - 1):

            @pl.when(reaches(peers[i], t) if arriving else reaches(t, peers[i]))
            def _():
                act(sends(i, peers[i] if arriving else t))

    def row_sends(top, bottom, first, last, above, below, top_send, bottom_send, recv):
        up_peer, down_peer = lax.rem(t + n - 1, n), lax.rem(t + 1, n)
        return (
            [remote(top, first, top_send.at[i], recv.at[0], p) for i, p in enumerate(peers)],
            [remote(bottom, last, bottom_send.at[i], recv.at[1], p) for i, p in enumerate(peers)],
            remote(top, below, top_send.at[n], recv.at[2], up_peer),
            remote(bottom, above, bottom_send.at[n], recv.at[3], down_peer),
        )

    lines = row_sends(
        scaling.at[:, pl.ds(0, DEPTH), :], scaling.at[:, pl.ds(rows - DEPTH, DEPTH), :],
        first, last, above, below, top_send, bottom_send, row_recv,
    )
    lines_d = row_sends(
        top_d, bottom_d, first_d, last_d, above_d, below_d, top_send_d, bottom_send_d, row_recv_d
    )

    def on_rows(sends, act):
        to_first, to_last, to_above, to_below = sends

        @pl.when(t == 0)
        def _():
            for copy in reversed(to_first):
                act(copy)

        @pl.when(t == n - 1)
        def _():
            for copy in to_last:
                act(copy)

        @pl.when(t > 0)
        def _():
            act(to_above)

        @pl.when(t < n - 1)
        def _():
            act(to_below)

    def receive_rows(sends):
        to_first, to_last, to_above, to_below = sends

        @pl.when(t > 0)
        def _():
            to_first[0].wait_recv()
            to_below.wait_recv()

        @pl.when(t < n - 1)
        def _():
            to_last[0].wait_recv()
            to_above.wait_recv()

    pl.semaphore_wait(barrier, n - 1 + members - 1)

    on_packs(send_pack, lambda copy: copy.start(), False)
    on_rows(lines, lambda copy: copy.start())

    load_density.wait()
    turned = turned_columns(density, 0)
    other = turned if blocks == 1 else turned_columns(density, side - LANES)
    pack_d[...] = jnp.where(sub8 < 4, turned[:8], other[LANES - 8 :])
    packs_d[t] = pack_d[...]
    for j in range(pairs):
        top_d[j] = jnp.where(
            sub < 4, density[2 * j, :8, :], pltpu.roll(density[2 * j + 1, :8, :], 4, 0)
        )
        bottom_d[j] = jnp.where(
            sub >= 4, density[2 * j, rows - 8 :, :], pltpu.roll(density[2 * j + 1, rows - 8 :, :], 4, 0)
        )
    on_packs(send_pack_d, lambda copy: copy.start(), False)
    on_rows(lines_d, lambda copy: copy.start())

    def send_weight(i, slot):
        return remote(
            mine, weights.at[slot], weight_send.at[i], weight_recv.at[slot], partners[i], "member"
        )

    for i in range(members - 1):
        send_weight(i, m).start()

    @pl.when(t == 0)
    def _():
        first[...] = scaling[:, :DEPTH, :]
        first_d[...] = top_d[...]
        above[...] = jnp.ones(above.shape, jnp.float32)
        above_d[...] = jnp.ones(above_d.shape, jnp.float32)

    @pl.when(t == n - 1)
    def _():
        last[...] = scaling[:, rows - DEPTH :, :]
        last_d[...] = bottom_d[...]
        below[...] = jnp.ones(below.shape, jnp.float32)
        below_d[...] = jnp.ones(below_d.shape, jnp.float32)

    ghosts[...] = jnp.zeros(ghosts.shape, jnp.float32)
    ghost_columns[...] = jnp.zeros(ghost_columns.shape, jnp.float32)

    whole_line, merged_line = {}, {}
    row_of = lax.broadcasted_iota(jnp.int32, (24, LANES), 0)
    flipped = jnp.zeros((24, LANES), jnp.int32)
    for f in range(faces):
        for e in range(4):
            face, edge = seams_ref[0, e, f], seams_ref[1, e, f]
            second = lax.rem(edge, 2)
            whole_line[f, e] = 32 * face + 8 * edge + 7 * second
            merged_line[f, e] = 16 * face + 4 * (edge - second) + 7 * second
            flipped = jnp.where(row_of == 4 * f + 3 - e, seams_ref[2, e, f], flipped)
    turns = flipped == 1

    def gather_strip(read, f):
        parts = []
        for b in range(blocks):
            out = jnp.ones((8, LANES), jnp.float32)
            for k in range(per_block):
                shift = (rows * (k - f)) % LANES
                piece = read(b * per_block + k)
                piece = pltpu.roll(piece, shift, 1) if shift else piece
                out = jnp.where((lane8 >= rows * k) & (lane8 < rows * (k + 1)), piece, out)
            parts.append(out)
        return parts[0] if blocks == 1 else jnp.concatenate(parts, axis=1)

    on_packs(send_pack, lambda copy: copy.wait_recv(), True)
    for f in range(faces):
        for k in range(2):
            at = 32 * f + 16 + 8 * k
            strips[at : at + 8, :] = gather_strip(lambda s: packs[s, k], f)
    receive_rows(lines)
    for f in range(faces):
        strips[32 * f : 32 * f + 8, :] = first[f]
        strips[32 * f + 8 : 32 * f + 16, :] = last[f]
        tile[f, :8] = above[f]
        tile[f, 8 : 8 + rows] = scaling[f]
        tile[f, 8 + rows :] = below[f]

    start = pl.multiple_of(rows * t, 8)
    reverse = LANES - 1 - lane8
    at_top = (sub == 7) & (t == 0)
    at_bottom = (sub == 0) & (t == n - 1)
    height = (rows + 16) // 8

    def place(line, shift):
        line = pltpu.roll(line, (LANES - shift) % LANES, 1)
        return line if blocks == 1 else jnp.concatenate([line] * blocks, axis=1)

    def stencil(u, up, down, ends):
        left = jnp.where(lane == 0, ends, pltpu.roll(u, 1, 1))
        right = jnp.where(lane == side - 1, ends, pltpu.roll(u, side - 1, 1))
        return u + KAPPA * (((up + down) + (left + right)) - 4.0 * u)

    def read_ghosts(line_of):
        for f in range(faces):
            for e in range(4):
                row = 4 * f + 3 - e
                ghosts[row : row + 1, :] = strips[pl.ds(line_of[f, e], 1), :]
        lines = [ghosts[: 4 * faces, b * LANES : (b + 1) * LANES] for b in range(blocks)]
        rest = jnp.zeros((32 - 4 * faces, LANES), jnp.float32)
        for b in range(blocks):
            backward = jnp.concatenate(
                [
                    jnp.take_along_axis(
                        lines[blocks - 1 - b][r : r + 8], reverse, axis=1, mode="promise_in_bounds"
                    )
                    for r in range(0, 4 * faces, 8)
                ],
                axis=0,
            )
            line = jnp.where(turns, backward, lines[b])
            ghosts[: 4 * faces, b * LANES : (b + 1) * LANES] = line
            at = 8 + b * LANES
            ghost_columns[at : at + LANES, :32] = jnp.concatenate([line, rest], axis=0).T

    def ghost_row(f, e):
        row = 4 * f + 3 - e
        return jnp.broadcast_to(ghosts[row : row + 1, :], (8, side))

    def advance(u, first_rows, last_rows, over, under, columns, shift):
        up, down = first_rows, last_rows
        if over is not None:
            up = jnp.where(sub == 0, over, up)
        if under is not None:
            down = jnp.where(sub == 7, under, down)
        return stencil(u, up, down, place(columns, shift))

    def advance_tile(f, u, columns, closed):
        count = len(u)
        ups = [pltpu.roll(v, 1, 0) for v in u]
        downs = [pltpu.roll(v, 7, 0) for v in u]
        result = []
        for j in range(count):
            before = ups[j - 1] if j or closed else None
            after = downs[(j + 1) % count] if j < count - 1 or closed else None
            result.append(advance(u[j], ups[j], downs[j], before, after, columns[j], 4 * f + 1))
        return result

    def diffuse(step, carry):
        read_ghosts(whole_line)
        ends = (ghost_columns[8:16, :], ghost_columns[side : side + 8, :])
        for f in range(faces):
            for e in range(4):
                at = 32 * f + 8 * e
                u = strips[at : at + 8, :]
                ghost = ghost_row(f, e)
                over, under = (None, ghost) if e % 2 else (ghost, None)
                strips[at : at + 8, :] = advance(
                    u, pltpu.roll(u, 1, 0), pltpu.roll(u, 7, 0), over, under,
                    ends[e % 2], 4 * f + 1 + (e // 2) * 2,
                )
        for f in range(faces):
            u = [tile[f, 8 * j : 8 * j + 8, :] for j in range(height)]
            u[0] = jnp.where(at_top, ghost_row(f, 0), u[0])
            u[-1] = jnp.where(at_bottom, ghost_row(f, 1), u[-1])
            columns = [ghost_columns[pl.ds(start + 8 * j, 8), :] for j in range(height)]
            for j, value in enumerate(advance_tile(f, u, columns, False)):
                tile[f, 8 * j : 8 * j + 8, :] = value
        return carry

    def diffuse_merged(step, carry):
        read_ghosts(merged_line)
        ends = jnp.where(sub8 < 4, ghost_columns[8:16, :], ghost_columns[side : side + 8, :])
        for f in range(faces):
            for k in range(2):
                at = 16 * f + 8 * k
                u = strips[at : at + 8, :]
                strips[at : at + 8, :] = advance(
                    u, pltpu.roll(u, 1, 0), pltpu.roll(u, 7, 0),
                    ghost_row(f, 2 * k), ghost_row(f, 2 * k + 1), ends, 4 * f + 1 + 2 * k,
                )
        columns = [ghost_columns[pl.ds(start + 8 * j, 8), :] for j in range(height)]
        columns = columns[1:-1] + [jnp.where(sub8 < 4, columns[-1], columns[0])]
        for f in range(faces):
            u = [tile[f, 8 * j : 8 * j + 8, :] for j in range(1, height)]
            u[-1] = jnp.where(at_top, ghost_row(f, 0), u[-1])
            u[-1] = jnp.where(at_bottom, ghost_row(f, 1), u[-1])
            for j, value in enumerate(advance_tile(f, u, columns, True)):
                tile[f, 8 * j + 8 : 8 * j + 16, :] = value
        return carry

    lax.fori_loop(0, STEPS, diffuse, 0)

    on_packs(send_pack_d, lambda copy: copy.wait_recv(), True)
    receive_rows(lines_d)
    upper = sub < 4
    for f in range(faces):
        turn = (lambda v: v) if f % 2 == 0 else (lambda v: pltpu.roll(v, 4, 0))
        whole = [strips[32 * f + 8 * e : 32 * f + 8 * e + 8, :] for e in range(4)]
        edge_rows = jnp.where(upper, turn(first_d[f // 2]), turn(last_d[f // 2]))
        edge_columns = gather_strip(lambda s: packs_d[s], f)
        strips[16 * f : 16 * f + 8, :] = edge_rows / jnp.where(upper, whole[0], whole[1])
        strips[16 * f + 8 : 16 * f + 16, :] = edge_columns / jnp.where(upper, whole[2], whole[3])
        around = jnp.where(upper, turn(below_d[f // 2]), turn(above_d[f // 2]))
        dual = density[f] / tile[f, 8 : 8 + rows, :]
        tile[f, 8 + rows :, :] = around / jnp.where(upper, tile[f, 8 + rows :, :], tile[f, :8, :])
        tile[f, 8 : 8 + rows, :] = dual
        results[1, f] = dual
    store_dual = pltpu.make_async_copy(results.at[1], out_hbm.at[1], local.at[2])
    store_dual.start()
    lax.fori_loop(0, STEPS, diffuse_merged, 0)

    marginal = scaling[...] * tile[:, 8 : 8 + rows, :]
    logs[...] = weight_ref[0] * jnp.log(marginal)

    def send_logs(i, slot):
        return remote(logs, others.at[slot], log_send.at[i], log_recv.at[slot], partners[i], "member")

    for i in range(members - 1):
        send_logs(i, m).start()
    weight = mine[...]
    for i in range(members - 1):
        send_weight(i, partners[i]).wait_recv()
        weight = weight + weights[partners[i]]
    if blocks > 1:
        weight = jnp.concatenate([weight] * blocks, axis=1)
    total = logs[...]
    for i in range(members - 1):
        send_logs(i, partners[i]).wait_recv()
        total = total + others[partners[i]]
    bary = jnp.exp(total / weight[:1].reshape(1, 1, side))
    results[2] = bary
    store_bary = pltpu.make_async_copy(results.at[2], out_hbm.at[2], local.at[1])
    store_bary.start()
    results[0] = (scaling[...] * bary) / marginal
    store_new = pltpu.make_async_copy(results.at[0], out_hbm.at[0], local.at[0])
    store_new.start()

    for i in range(members - 1):
        send_logs(i, m).wait_send()
        send_weight(i, m).wait_send()
    on_packs(send_pack, lambda copy: copy.wait_send(), False)
    on_packs(send_pack_d, lambda copy: copy.wait_send(), False)
    on_rows(lines, lambda copy: copy.wait_send())
    on_rows(lines_d, lambda copy: copy.wait_send())
    store_dual.wait()
    store_bary.wait()
    store_new.wait()


def hand_out(results, new_hbm, dual_hbm, bary_hbm, held, loaded, stored):
    targets = (new_hbm.at[0], dual_hbm.at[0], bary_hbm)
    loads = [pltpu.make_async_copy(results.at[i], held.at[i], loaded.at[i]) for i in range(3)]
    stores = [pltpu.make_async_copy(held.at[i], targets[i], stored.at[i]) for i in range(3)]
    for load in loads:
        load.start()
    for load, store in zip(loads, stores):
        load.wait()
        store.start()
    for store in stores:
        store.wait()


def body(density, scaling, member_weights, seams):
    n = lax.axis_size("tile")
    members = lax.axis_size("member")
    _, faces, rows, side = scaling.shape
    vmem = lambda *shape: pltpu.VMEM(shape, jnp.float32)
    dma = lambda count: pltpu.SemaphoreType.DMA((count,))
    smem = pl.BlockSpec(memory_space=pltpu.SMEM)
    hbm = pl.BlockSpec(memory_space=pltpu.HBM)
    results = pl.pallas_call(
        functools.partial(kernel, n, members, faces, rows, side),
        out_shape=jax.ShapeDtypeStruct((3, faces, rows, side), jnp.float32),
        in_specs=[smem, smem, hbm, hbm],
        out_specs=hbm,
        scratch_shapes=[
            vmem(faces, rows, side),
            vmem(faces, rows, side),
            vmem(32 * faces, side),
            vmem(faces, rows + 16, side),
            vmem(32, side),
            vmem(side + 16, LANES),
            vmem(3, faces, rows, side),
            vmem(2, 8, LANES),
            vmem(n, 2, 8, LANES),
            *[vmem(faces, DEPTH, side)] * 4,
            vmem(8, LANES),
            vmem(n, 8, LANES),
            *[vmem(faces // 2, 8, side)] * 6,
            vmem(faces, rows, side),
            vmem(members, faces, rows, side),
            vmem(8, LANES),
            vmem(members, 8, LANES),
            dma(3), dma(n), dma(n), dma(n), dma(n),
            dma(n + 1), dma(n + 1), dma(4), dma(n + 1), dma(n + 1), dma(4),
            dma(members), dma(members), dma(members), dma(members),
        ],
        compiler_params=pltpu.CompilerParams(
            collective_id=0, has_side_effects=True
        ),
    )(seams, member_weights, density, scaling)
    return pl.pallas_call(
        hand_out,
        out_shape=(
            jax.ShapeDtypeStruct(scaling.shape, jnp.float32),
            jax.ShapeDtypeStruct(scaling.shape, jnp.float32),
            jax.ShapeDtypeStruct(scaling.shape[1:], jnp.float32),
        ),
        in_specs=[hbm],
        out_specs=(hbm, hbm, hbm),
        scratch_shapes=[vmem(3, faces, rows, side), dma(3), dma(3)],
    )(results)


def solution(mesh):
    return jax.shard_map(
        body,
        mesh=mesh,
        in_specs=(
            P("member", None, "tile", None),
            P("member", None, "tile", None),
            P("member"),
            P(),
        ),
        out_specs=(
            P("member", None, "tile", None),
            P("member", None, "tile", None),
            P(None, "tile", None),
        ),
        check_vma=False,
    )
```

```python
import functools

import jax
import jax.numpy as jnp
from jax import lax
from jax.experimental import pallas as pl
from jax.experimental.pallas import tpu as pltpu
from jax.sharding import PartitionSpec as P

STEPS = 4
KAPPA = 0.24
LANES = 128
DEPTH = 8
MESH = pl.DeviceIdType.MESH


def kernel(
    n, members, faces, rows, side,
    seams_hbm, weight_hbm, density_hbm, scaling_hbm,
    out_hbm,
    seams_ref, weight_ref, density, scaling, strips, tile, ghosts, ghost_columns, results,
    pack, packs, first, last, above, below,
    pack_d, packs_d, top_d, bottom_d, first_d, last_d, above_d, below_d,
    logs, others, mine, weights,
    local, pack_send, pack_recv, pack_send_d, pack_recv_d,
    top_send, bottom_send, row_recv, top_send_d, bottom_send_d, row_recv_d,
    log_send, log_recv, weight_send, weight_recv,
):
    t = lax.axis_index("tile")
    m = lax.axis_index("member")
    blocks = side // LANES
    per_block = LANES // rows
    pairs = faces // 2

    packs[...] = jnp.ones(packs.shape, jnp.float32)
    packs_d[...] = jnp.ones(packs_d.shape, jnp.float32)

    barrier = pltpu.get_barrier_semaphore()
    for i in range(1, n):
        pl.semaphore_signal(barrier, inc=1, device_id={"tile": lax.rem(t + i, n)}, device_id_type=MESH)
    for i in range(1, members):
        pl.semaphore_signal(
            barrier, inc=1, device_id={"member": lax.rem(m + i, members)}, device_id_type=MESH
        )
    load_scaling = pltpu.make_async_copy(scaling_hbm.at[0], scaling, local.at[0])
    load_density = pltpu.make_async_copy(density_hbm.at[0], density, local.at[1])
    load_scaling.start()
    load_density.start()
    load_weight = pltpu.make_async_copy(weight_hbm, weight_ref, local.at[3])
    load_seams = pltpu.make_async_copy(seams_hbm, seams_ref, local.at[4])
    load_weight.start()
    load_seams.start()

    sub8 = lax.broadcasted_iota(jnp.int32, (8, LANES), 0)
    lane8 = lax.broadcasted_iota(jnp.int32, (8, LANES), 1)
    sub = lax.broadcasted_iota(jnp.int32, (8, side), 0)
    lane = lax.broadcasted_iota(jnp.int32, (8, side), 1)

    def turned_columns(src, at):
        flat = src[:, :, at : at + LANES].reshape(faces * rows, LANES)
        rest = jnp.ones((LANES - faces * rows, LANES), jnp.float32)
        return jnp.concatenate([flat, rest], axis=0).T


    peers = [lax.rem(t + i, n) for i in range(1, n)]
    partners = [lax.rem(m + i, members) for i in range(1, members)]

    def remote(src, dst, send, recv, peer, axis="tile"):
        return pltpu.make_async_remote_copy(
            src_ref=src, dst_ref=dst, send_sem=send, recv_sem=recv,
            device_id={axis: peer}, device_id_type=MESH,
        )

    def send_pack(i, slot):
        return remote(pack, packs.at[slot], pack_send.at[i], pack_recv.at[slot], peers[i])

    def send_pack_d(i, slot):
        return remote(pack_d, packs_d.at[slot], pack_send_d.at[i], pack_recv_d.at[slot], peers[i])

    def reaches(source, target):
        mirror = n - 1 - target
        ends = (target == 0) | (target == n - 1)
        return ends | (jnp.abs(source - target) <= 1) | (jnp.abs(source - mirror) <= 1)

    def on_packs(sends, act, arriving):
        for i in range(n - 1):

            @pl.when(reaches(peers[i], t) if arriving else reaches(t, peers[i]))
            def _():
                act(sends(i, peers[i] if arriving else t))

    def row_sends(top, bottom, first, last, above, below, top_send, bottom_send, recv):
        up_peer, down_peer = lax.rem(t + n - 1, n), lax.rem(t + 1, n)
        return (
            [remote(top, first, top_send.at[i], recv.at[0], p) for i, p in enumerate(peers)],
            [remote(bottom, last, bottom_send.at[i], recv.at[1], p) for i, p in enumerate(peers)],
            remote(top, below, top_send.at[n], recv.at[2], up_peer),
            remote(bottom, above, bottom_send.at[n], recv.at[3], down_peer),
        )

    lines = row_sends(
        scaling.at[:, pl.ds(0, DEPTH), :], scaling.at[:, pl.ds(rows - DEPTH, DEPTH), :],
        first, last, above, below, top_send, bottom_send, row_recv,
    )
    lines_d = row_sends(
        top_d, bottom_d, first_d, last_d, above_d, below_d, top_send_d, bottom_send_d, row_recv_d
    )

    def on_rows(sends, act):
        to_first, to_last, to_above, to_below = sends

        @pl.when(t == 0)
        def _():
            for copy in reversed(to_first):
                act(copy)

        @pl.when(t == n - 1)
        def _():
            for copy in to_last:
                act(copy)

        @pl.when(t > 0)
        def _():
            act(to_above)

        @pl.when(t < n - 1)
        def _():
            act(to_below)

    def receive_rows(sends):
        to_first, to_last, to_above, to_below = sends

        @pl.when(t > 0)
        def _():
            to_first[0].wait_recv()
            to_below.wait_recv()

        @pl.when(t < n - 1)
        def _():
            to_last[0].wait_recv()
            to_above.wait_recv()

    load_scaling.wait()
    turned = turned_columns(scaling, 0)
    pack[0] = turned[:8]
    pack[1] = (turned if blocks == 1 else turned_columns(scaling, side - LANES))[LANES - 8 :]
    packs[t] = pack[...]
    load_density.wait()
    turned = turned_columns(density, 0)
    other = turned if blocks == 1 else turned_columns(density, side - LANES)
    pack_d[...] = jnp.where(sub8 < 4, turned[:8], other[LANES - 8 :])
    packs_d[t] = pack_d[...]
    for j in range(pairs):
        top_d[j] = jnp.where(
            sub < 4, density[2 * j, :8, :], pltpu.roll(density[2 * j + 1, :8, :], 4, 0)
        )
        bottom_d[j] = jnp.where(
            sub >= 4, density[2 * j, rows - 8 :, :], pltpu.roll(density[2 * j + 1, rows - 8 :, :], 4, 0)
        )
    pl.semaphore_wait(barrier, n - 1 + members - 1)

    on_packs(send_pack, lambda copy: copy.start(), False)
    on_rows(lines, lambda copy: copy.start())

    on_packs(send_pack_d, lambda copy: copy.start(), False)
    on_rows(lines_d, lambda copy: copy.start())

    def send_weight(i, slot):
        return remote(
            mine, weights.at[slot], weight_send.at[i], weight_recv.at[slot], partners[i], "member"
        )

    load_weight.wait()
    mine[...] = jnp.full((8, LANES), weight_ref[0], jnp.float32)
    for i in range(members - 1):
        send_weight(i, m).start()

    @pl.when(t == 0)
    def _():
        first[...] = scaling[:, :DEPTH, :]
        first_d[...] = top_d[...]
        above[...] = jnp.ones(above.shape, jnp.float32)
        above_d[...] = jnp.ones(above_d.shape, jnp.float32)

    @pl.when(t == n - 1)
    def _():
        last[...] = scaling[:, rows - DEPTH :, :]
        last_d[...] = bottom_d[...]
        below[...] = jnp.ones(below.shape, jnp.float32)
        below_d[...] = jnp.ones(below_d.shape, jnp.float32)

    ghosts[...] = jnp.zeros(ghosts.shape, jnp.float32)
    ghost_columns[...] = jnp.zeros(ghost_columns.shape, jnp.float32)

    load_seams.wait()
    whole_line, merged_line = {}, {}
    row_of = lax.broadcasted_iota(jnp.int32, (24, LANES), 0)
    flipped = jnp.zeros((24, LANES), jnp.int32)
    for f in range(faces):
        for e in range(4):
            face, edge = seams_ref[0, e, f], seams_ref[1, e, f]
            second = lax.rem(edge, 2)
            whole_line[f, e] = 32 * face + 8 * edge + 7 * second
            merged_line[f, e] = 16 * face + 4 * (edge - second) + 7 * second
            flipped = jnp.where(row_of == 4 * f + 3 - e, seams_ref[2, e, f], flipped)
    turns = flipped == 1

    def gather_strip(read, f):
        parts = []
        for b in range(blocks):
            out = jnp.ones((8, LANES), jnp.float32)
            for k in range(per_block):
                shift = (rows * (k - f)) % LANES
                piece = read(b * per_block + k)
                piece = pltpu.roll(piece, shift, 1) if shift else piece
                out = jnp.where((lane8 >= rows * k) & (lane8 < rows * (k + 1)), piece, out)
            parts.append(out)
        return parts[0] if blocks == 1 else jnp.concatenate(parts, axis=1)

    on_packs(send_pack, lambda copy: copy.wait_recv(), True)
    for f in range(faces):
        for k in range(2):
            at = 32 * f + 16 + 8 * k
            strips[at : at + 8, :] = gather_strip(lambda s: packs[s, k], f)
    receive_rows(lines)
    for f in range(faces):
        strips[32 * f : 32 * f + 8, :] = first[f]
        strips[32 * f + 8 : 32 * f + 16, :] = last[f]
        tile[f, :8] = above[f]
        tile[f, 8 : 8 + rows] = scaling[f]
        tile[f, 8 + rows :] = below[f]

    start = pl.multiple_of(rows * t, 8)
    reverse = LANES - 1 - lane8
    at_top = (sub == 7) & (t == 0)
    at_bottom = (sub == 0) & (t == n - 1)
    height = (rows + 16) // 8

    def place(line, shift):
        line = pltpu.roll(line, (LANES - shift) % LANES, 1)
        return line if blocks == 1 else jnp.concatenate([line] * blocks, axis=1)

    def stencil(u, up, down, ends):
        left = jnp.where(lane == 0, ends, pltpu.roll(u, 1, 1))
        right = jnp.where(lane == side - 1, ends, pltpu.roll(u, side - 1, 1))
        return u + KAPPA * (((up + down) + (left + right)) - 4.0 * u)

    def read_ghosts(line_of):
        for f in range(faces):
            for e in range(4):
                row = 4 * f + 3 - e
                ghosts[row : row + 1, :] = strips[pl.ds(line_of[f, e], 1), :]
        lines = [ghosts[: 4 * faces, b * LANES : (b + 1) * LANES] for b in range(blocks)]
        rest = jnp.zeros((32 - 4 * faces, LANES), jnp.float32)
        for b in range(blocks):
            backward = jnp.concatenate(
                [
                    jnp.take_along_axis(
                        lines[blocks - 1 - b][r : r + 8], reverse, axis=1, mode="promise_in_bounds"
                    )
                    for r in range(0, 4 * faces, 8)
                ],
                axis=0,
            )
            line = jnp.where(turns, backward, lines[b])
            ghosts[: 4 * faces, b * LANES : (b + 1) * LANES] = line
            at = 8 + b * LANES
            ghost_columns[at : at + LANES, :32] = jnp.concatenate([line, rest], axis=0).T

    def ghost_row(f, e):
        row = 4 * f + 3 - e
        return jnp.broadcast_to(ghosts[row : row + 1, :], (8, side))

    def advance(u, first_rows, last_rows, over, under, columns, shift):
        up, down = first_rows, last_rows
        if over is not None:
            up = jnp.where(sub == 0, over, up)
        if under is not None:
            down = jnp.where(sub == 7, under, down)
        return stencil(u, up, down, place(columns, shift))

    def advance_tile(f, u, columns, closed):
        count = len(u)
        ups = [pltpu.roll(v, 1, 0) for v in u]
        downs = [pltpu.roll(v, 7, 0) for v in u]
        result = []
        for j in range(count):
            before = ups[j - 1] if j or closed else None
            after = downs[(j + 1) % count] if j < count - 1 or closed else None
            result.append(advance(u[j], ups[j], downs[j], before, after, columns[j], 4 * f + 1))
        return result

    def diffuse(step, carry):
        read_ghosts(whole_line)
        ends = (ghost_columns[8:16, :], ghost_columns[side : side + 8, :])
        for f in range(faces):
            for e in range(4):
                at = 32 * f + 8 * e
                u = strips[at : at + 8, :]
                ghost = ghost_row(f, e)
                over, under = (None, ghost) if e % 2 else (ghost, None)
                strips[at : at + 8, :] = advance(
                    u, pltpu.roll(u, 1, 0), pltpu.roll(u, 7, 0), over, under,
                    ends[e % 2], 4 * f + 1 + (e // 2) * 2,
                )
        for f in range(faces):
            u = [tile[f, 8 * j : 8 * j + 8, :] for j in range(height)]
            u[0] = jnp.where(at_top, ghost_row(f, 0), u[0])
            u[-1] = jnp.where(at_bottom, ghost_row(f, 1), u[-1])
            columns = [ghost_columns[pl.ds(start + 8 * j, 8), :] for j in range(height)]
            for j, value in enumerate(advance_tile(f, u, columns, False)):
                tile[f, 8 * j : 8 * j + 8, :] = value
        return carry

    def diffuse_merged(step, carry):
        read_ghosts(merged_line)
        ends = jnp.where(sub8 < 4, ghost_columns[8:16, :], ghost_columns[side : side + 8, :])
        for f in range(faces):
            for k in range(2):
                at = 16 * f + 8 * k
                u = strips[at : at + 8, :]
                strips[at : at + 8, :] = advance(
                    u, pltpu.roll(u, 1, 0), pltpu.roll(u, 7, 0),
                    ghost_row(f, 2 * k), ghost_row(f, 2 * k + 1), ends, 4 * f + 1 + 2 * k,
                )
        columns = [ghost_columns[pl.ds(start + 8 * j, 8), :] for j in range(height)]
        columns = columns[1:-1] + [jnp.where(sub8 < 4, columns[-1], columns[0])]
        for f in range(faces):
            u = [tile[f, 8 * j : 8 * j + 8, :] for j in range(1, height)]
            u[-1] = jnp.where(at_top, ghost_row(f, 0), u[-1])
            u[-1] = jnp.where(at_bottom, ghost_row(f, 1), u[-1])
            for j, value in enumerate(advance_tile(f, u, columns, True)):
                tile[f, 8 * j + 8 : 8 * j + 16, :] = value
        return carry

    lax.fori_loop(0, STEPS, diffuse, 0)

    on_packs(send_pack_d, lambda copy: copy.wait_recv(), True)
    receive_rows(lines_d)
    upper = sub < 4
    for f in range(faces):
        turn = (lambda v: v) if f % 2 == 0 else (lambda v: pltpu.roll(v, 4, 0))
        whole = [strips[32 * f + 8 * e : 32 * f + 8 * e + 8, :] for e in range(4)]
        edge_rows = jnp.where(upper, turn(first_d[f // 2]), turn(last_d[f // 2]))
        edge_columns = gather_strip(lambda s: packs_d[s], f)
        strips[16 * f : 16 * f + 8, :] = edge_rows / jnp.where(upper, whole[0], whole[1])
        strips[16 * f + 8 : 16 * f + 16, :] = edge_columns / jnp.where(upper, whole[2], whole[3])
        around = jnp.where(upper, turn(below_d[f // 2]), turn(above_d[f // 2]))
        dual = density[f] / tile[f, 8 : 8 + rows, :]
        tile[f, 8 + rows :, :] = around / jnp.where(upper, tile[f, 8 + rows :, :], tile[f, :8, :])
        tile[f, 8 : 8 + rows, :] = dual
        results[1, f] = dual
    store_dual = pltpu.make_async_copy(results.at[1], out_hbm.at[1], local.at[2])
    store_dual.start()
    lax.fori_loop(0, STEPS, diffuse_merged, 0)

    marginal = scaling[...] * tile[:, 8 : 8 + rows, :]
    logs[...] = weight_ref[0] * jnp.log(marginal)

    def send_logs(i, slot):
        return remote(logs, others.at[slot], log_send.at[i], log_recv.at[slot], partners[i], "member")

    for i in range(members - 1):
        send_logs(i, m).start()
    weight = mine[...]
    for i in range(members - 1):
        send_weight(i, partners[i]).wait_recv()
        weight = weight + weights[partners[i]]
    if blocks > 1:
        weight = jnp.concatenate([weight] * blocks, axis=1)
    total = logs[...]
    for i in range(members - 1):
        send_logs(i, partners[i]).wait_recv()
        total = total + others[partners[i]]
    bary = jnp.exp(total / weight[:1].reshape(1, 1, side))
    results[2] = bary
    store_bary = pltpu.make_async_copy(results.at[2], out_hbm.at[2], local.at[1])
    store_bary.start()
    results[0] = (scaling[...] * bary) / marginal
    store_new = pltpu.make_async_copy(results.at[0], out_hbm.at[0], local.at[0])
    store_new.start()

    for i in range(members - 1):
        send_logs(i, m).wait_send()
        send_weight(i, m).wait_send()
    on_packs(send_pack, lambda copy: copy.wait_send(), False)
    on_packs(send_pack_d, lambda copy: copy.wait_send(), False)
    on_rows(lines, lambda copy: copy.wait_send())
    on_rows(lines_d, lambda copy: copy.wait_send())
    store_dual.wait()
    store_bary.wait()
    store_new.wait()


def hand_out(results, new_hbm, dual_hbm, bary_hbm, held, loaded, stored):
    targets = (new_hbm.at[0], dual_hbm.at[0], bary_hbm)
    loads = [pltpu.make_async_copy(results.at[i], held.at[i], loaded.at[i]) for i in range(3)]
    stores = [pltpu.make_async_copy(held.at[i], targets[i], stored.at[i]) for i in range(3)]
    for load in loads:
        load.start()
    for load, store in zip(loads, stores):
        load.wait()
        store.start()
    for store in stores:
        store.wait()


def body(density, scaling, member_weights, seams):
    n = lax.axis_size("tile")
    members = lax.axis_size("member")
    _, faces, rows, side = scaling.shape
    vmem = lambda *shape: pltpu.VMEM(shape, jnp.float32)
    dma = lambda count: pltpu.SemaphoreType.DMA((count,))
    hbm = pl.BlockSpec(memory_space=pltpu.HBM)
    results = pl.pallas_call(
        functools.partial(kernel, n, members, faces, rows, side),
        out_shape=jax.ShapeDtypeStruct((3, faces, rows, side), jnp.float32),
        in_specs=[hbm] * 4,
        out_specs=hbm,
        scratch_shapes=[
            pltpu.SMEM(seams.shape, jnp.int32),
            pltpu.SMEM(member_weights.shape, jnp.float32),
            vmem(faces, rows, side),
            vmem(faces, rows, side),
            vmem(32 * faces, side),
            vmem(faces, rows + 16, side),
            vmem(32, side),
            vmem(side + 16, LANES),
            vmem(3, faces, rows, side),
            vmem(2, 8, LANES),
            vmem(n, 2, 8, LANES),
            *[vmem(faces, DEPTH, side)] * 4,
            vmem(8, LANES),
            vmem(n, 8, LANES),
            *[vmem(faces // 2, 8, side)] * 6,
            vmem(faces, rows, side),
            vmem(members, faces, rows, side),
            vmem(8, LANES),
            vmem(members, 8, LANES),
            dma(5), dma(n), dma(n), dma(n), dma(n),
            dma(n + 1), dma(n + 1), dma(4), dma(n + 1), dma(n + 1), dma(4),
            dma(members), dma(members), dma(members), dma(members),
        ],
        compiler_params=pltpu.CompilerParams(
            collective_id=0, has_side_effects=True
        ),
    )(seams, member_weights, density, scaling)
    return pl.pallas_call(
        hand_out,
        out_shape=(
            jax.ShapeDtypeStruct(scaling.shape, jnp.float32),
            jax.ShapeDtypeStruct(scaling.shape, jnp.float32),
            jax.ShapeDtypeStruct(scaling.shape[1:], jnp.float32),
        ),
        in_specs=[hbm],
        out_specs=(hbm, hbm, hbm),
        scratch_shapes=[vmem(3, faces, rows, side), dma(3), dma(3)],
    )(results)


def solution(mesh):
    return jax.shard_map(
        body,
        mesh=mesh,
        in_specs=(
            P("member", None, "tile", None),
            P("member", None, "tile", None),
            P("member"),
            P(),
        ),
        out_specs=(
            P("member", None, "tile", None),
            P("member", None, "tile", None),
            P(None, "tile", None),
        ),
        check_vma=False,
    )
```

```python
import functools

import jax
import jax.numpy as jnp
from jax import lax
from jax.experimental import pallas as pl
from jax.experimental.pallas import tpu as pltpu
from jax.sharding import PartitionSpec as P

STEPS = 4
KAPPA = 0.24
LANES = 128
DEPTH = 8
MESH = pl.DeviceIdType.MESH


def kernel(
    n, members, faces, rows, side,
    seams_hbm, weight_hbm, density_hbm, scaling_hbm,
    out_hbm,
    seams_ref, weight_ref, density, scaling, strips, tile, ghosts, ghost_columns, results,
    pack, packs, first, last, above, below,
    top_d, bottom_d, first_d, last_d, above_d, below_d,
    logs, others, mine, weights,
    local, pack_send, pack_recv,
    top_send, bottom_send, row_recv, top_send_d, bottom_send_d, row_recv_d,
    log_send, log_recv, weight_send, weight_recv,
):
    t = lax.axis_index("tile")
    m = lax.axis_index("member")
    blocks = side // LANES
    per_block = LANES // rows
    pairs = faces // 2

    packs[...] = jnp.ones(packs.shape, jnp.float32)

    barrier = pltpu.get_barrier_semaphore()
    for i in range(1, n):
        pl.semaphore_signal(barrier, inc=1, device_id={"tile": lax.rem(t + i, n)}, device_id_type=MESH)
    for i in range(1, members):
        pl.semaphore_signal(
            barrier, inc=1, device_id={"member": lax.rem(m + i, members)}, device_id_type=MESH
        )
    load_scaling = pltpu.make_async_copy(scaling_hbm.at[0], scaling, local.at[0])
    load_density = pltpu.make_async_copy(density_hbm.at[0], density, local.at[1])
    load_scaling.start()
    load_density.start()
    load_weight = pltpu.make_async_copy(weight_hbm, weight_ref, local.at[3])
    load_seams = pltpu.make_async_copy(seams_hbm, seams_ref, local.at[4])
    load_weight.start()
    load_seams.start()

    sub8 = lax.broadcasted_iota(jnp.int32, (8, LANES), 0)
    lane8 = lax.broadcasted_iota(jnp.int32, (8, LANES), 1)
    sub = lax.broadcasted_iota(jnp.int32, (8, side), 0)
    lane = lax.broadcasted_iota(jnp.int32, (8, side), 1)

    def turned_columns(src, at):
        flat = src[:, :, at : at + LANES].reshape(faces * rows, LANES)
        rest = jnp.ones((LANES - faces * rows, LANES), jnp.float32)
        return jnp.concatenate([flat, rest], axis=0).T


    peers = [lax.rem(t + i, n) for i in range(1, n)]
    partners = [lax.rem(m + i, members) for i in range(1, members)]

    def remote(src, dst, send, recv, peer, axis="tile"):
        return pltpu.make_async_remote_copy(
            src_ref=src, dst_ref=dst, send_sem=send, recv_sem=recv,
            device_id={axis: peer}, device_id_type=MESH,
        )

    def send_pack(i, slot):
        return remote(pack, packs.at[slot], pack_send.at[i], pack_recv.at[slot], peers[i])

    def reaches(source, target):
        mirror = n - 1 - target
        ends = (target == 0) | (target == n - 1)
        return ends | (jnp.abs(source - target) <= 1) | (jnp.abs(source - mirror) <= 1)

    def on_packs(sends, act, arriving):
        for i in range(n - 1):

            @pl.when(reaches(peers[i], t) if arriving else reaches(t, peers[i]))
            def _():
                act(sends(i, peers[i] if arriving else t))

    def row_sends(top, bottom, first, last, above, below, top_send, bottom_send, recv):
        up_peer, down_peer = lax.rem(t + n - 1, n), lax.rem(t + 1, n)
        return (
            [remote(top, first, top_send.at[i], recv.at[0], p) for i, p in enumerate(peers)],
            [remote(bottom, last, bottom_send.at[i], recv.at[1], p) for i, p in enumerate(peers)],
            remote(top, below, top_send.at[n], recv.at[2], up_peer),
            remote(bottom, above, bottom_send.at[n], recv.at[3], down_peer),
        )

    lines = row_sends(
        scaling.at[:, pl.ds(0, DEPTH), :], scaling.at[:, pl.ds(rows - DEPTH, DEPTH), :],
        first, last, above, below, top_send, bottom_send, row_recv,
    )
    lines_d = row_sends(
        top_d, bottom_d, first_d, last_d, above_d, below_d, top_send_d, bottom_send_d, row_recv_d
    )

    def on_rows(sends, act):
        to_first, to_last, to_above, to_below = sends

        @pl.when(t == 0)
        def _():
            for copy in reversed(to_first):
                act(copy)

        @pl.when(t == n - 1)
        def _():
            for copy in to_last:
                act(copy)

        @pl.when(t > 0)
        def _():
            act(to_above)

        @pl.when(t < n - 1)
        def _():
            act(to_below)

    def receive_rows(sends):
        to_first, to_last, to_above, to_below = sends

        @pl.when(t > 0)
        def _():
            to_first[0].wait_recv()
            to_below.wait_recv()

        @pl.when(t < n - 1)
        def _():
            to_last[0].wait_recv()
            to_above.wait_recv()

    load_scaling.wait()
    turned = turned_columns(scaling, 0)
    pack[0] = turned[:8]
    pack[1] = (turned if blocks == 1 else turned_columns(scaling, side - LANES))[LANES - 8 :]
    load_density.wait()
    turned = turned_columns(density, 0)
    other = turned if blocks == 1 else turned_columns(density, side - LANES)
    pack[2] = jnp.where(sub8 < 4, turned[:8], other[LANES - 8 :])
    packs[t] = pack[...]
    for j in range(pairs):
        top_d[j] = jnp.where(
            sub < 4, density[2 * j, :8, :], pltpu.roll(density[2 * j + 1, :8, :], 4, 0)
        )
        bottom_d[j] = jnp.where(
            sub >= 4, density[2 * j, rows - 8 :, :], pltpu.roll(density[2 * j + 1, rows - 8 :, :], 4, 0)
        )
    pl.semaphore_wait(barrier, n - 1 + members - 1)

    on_packs(send_pack, lambda copy: copy.start(), False)
    on_rows(lines, lambda copy: copy.start())

    on_rows(lines_d, lambda copy: copy.start())

    def send_weight(i, slot):
        return remote(
            mine, weights.at[slot], weight_send.at[i], weight_recv.at[slot], partners[i], "member"
        )

    load_weight.wait()
    mine[...] = jnp.full((8, LANES), weight_ref[0], jnp.float32)
    for i in range(members - 1):
        send_weight(i, m).start()

    @pl.when(t == 0)
    def _():
        first[...] = scaling[:, :DEPTH, :]
        first_d[...] = top_d[...]
        above[...] = jnp.ones(above.shape, jnp.float32)
        above_d[...] = jnp.ones(above_d.shape, jnp.float32)

    @pl.when(t == n - 1)
    def _():
        last[...] = scaling[:, rows - DEPTH :, :]
        last_d[...] = bottom_d[...]
        below[...] = jnp.ones(below.shape, jnp.float32)
        below_d[...] = jnp.ones(below_d.shape, jnp.float32)

    ghosts[...] = jnp.zeros(ghosts.shape, jnp.float32)
    ghost_columns[...] = jnp.zeros(ghost_columns.shape, jnp.float32)

    load_seams.wait()
    whole_line, merged_line = {}, {}
    row_of = lax.broadcasted_iota(jnp.int32, (24, LANES), 0)
    flipped = jnp.zeros((24, LANES), jnp.int32)
    for f in range(faces):
        for e in range(4):
            face, edge = seams_ref[0, e, f], seams_ref[1, e, f]
            second = lax.rem(edge, 2)
            whole_line[f, e] = 32 * face + 8 * edge + 7 * second
            merged_line[f, e] = 16 * face + 4 * (edge - second) + 7 * second
            flipped = jnp.where(row_of == 4 * f + 3 - e, seams_ref[2, e, f], flipped)
    turns = flipped == 1

    def gather_strip(read, f):
        parts = []
        for b in range(blocks):
            out = jnp.ones((8, LANES), jnp.float32)
            for k in range(per_block):
                shift = (rows * (k - f)) % LANES
                piece = read(b * per_block + k)
                piece = pltpu.roll(piece, shift, 1) if shift else piece
                out = jnp.where((lane8 >= rows * k) & (lane8 < rows * (k + 1)), piece, out)
            parts.append(out)
        return parts[0] if blocks == 1 else jnp.concatenate(parts, axis=1)

    on_packs(send_pack, lambda copy: copy.wait_recv(), True)
    for f in range(faces):
        for k in range(2):
            at = 32 * f + 16 + 8 * k
            strips[at : at + 8, :] = gather_strip(lambda s: packs[s, k], f)
    receive_rows(lines)
    for f in range(faces):
        strips[32 * f : 32 * f + 8, :] = first[f]
        strips[32 * f + 8 : 32 * f + 16, :] = last[f]
        tile[f, :8] = above[f]
        tile[f, 8 : 8 + rows] = scaling[f]
        tile[f, 8 + rows :] = below[f]

    start = pl.multiple_of(rows * t, 8)
    reverse = LANES - 1 - lane8
    at_top = (sub == 7) & (t == 0)
    at_bottom = (sub == 0) & (t == n - 1)
    height = (rows + 16) // 8

    def place(line, shift):
        line = pltpu.roll(line, (LANES - shift) % LANES, 1)
        return line if blocks == 1 else jnp.concatenate([line] * blocks, axis=1)

    def stencil(u, up, down, ends):
        left = jnp.where(lane == 0, ends, pltpu.roll(u, 1, 1))
        right = jnp.where(lane == side - 1, ends, pltpu.roll(u, side - 1, 1))
        return u + KAPPA * (((up + down) + (left + right)) - 4.0 * u)

    def read_ghosts(line_of):
        for f in range(faces):
            for e in range(4):
                row = 4 * f + 3 - e
                ghosts[row : row + 1, :] = strips[pl.ds(line_of[f, e], 1), :]
        lines = [ghosts[: 4 * faces, b * LANES : (b + 1) * LANES] for b in range(blocks)]
        rest = jnp.zeros((32 - 4 * faces, LANES), jnp.float32)
        for b in range(blocks):
            backward = jnp.concatenate(
                [
                    jnp.take_along_axis(
                        lines[blocks - 1 - b][r : r + 8], reverse, axis=1, mode="promise_in_bounds"
                    )
                    for r in range(0, 4 * faces, 8)
                ],
                axis=0,
            )
            line = jnp.where(turns, backward, lines[b])
            ghosts[: 4 * faces, b * LANES : (b + 1) * LANES] = line
            at = 8 + b * LANES
            ghost_columns[at : at + LANES, :32] = jnp.concatenate([line, rest], axis=0).T

    def ghost_row(f, e):
        row = 4 * f + 3 - e
        return jnp.broadcast_to(ghosts[row : row + 1, :], (8, side))

    def advance(u, first_rows, last_rows, over, under, columns, shift):
        up, down = first_rows, last_rows
        if over is not None:
            up = jnp.where(sub == 0, over, up)
        if under is not None:
            down = jnp.where(sub == 7, under, down)
        return stencil(u, up, down, place(columns, shift))

    def advance_tile(f, u, columns, closed):
        count = len(u)
        ups = [pltpu.roll(v, 1, 0) for v in u]
        downs = [pltpu.roll(v, 7, 0) for v in u]
        result = []
        for j in range(count):
            before = ups[j - 1] if j or closed else None
            after = downs[(j + 1) % count] if j < count - 1 or closed else None
            result.append(advance(u[j], ups[j], downs[j], before, after, columns[j], 4 * f + 1))
        return result

    def diffuse(step, carry):
        read_ghosts(whole_line)
        ends = (ghost_columns[8:16, :], ghost_columns[side : side + 8, :])
        for f in range(faces):
            for e in range(4):
                at = 32 * f + 8 * e
                u = strips[at : at + 8, :]
                ghost = ghost_row(f, e)
                over, under = (None, ghost) if e % 2 else (ghost, None)
                strips[at : at + 8, :] = advance(
                    u, pltpu.roll(u, 1, 0), pltpu.roll(u, 7, 0), over, under,
                    ends[e % 2], 4 * f + 1 + (e // 2) * 2,
                )
        for f in range(faces):
            u = [tile[f, 8 * j : 8 * j + 8, :] for j in range(height)]
            u[0] = jnp.where(at_top, ghost_row(f, 0), u[0])
            u[-1] = jnp.where(at_bottom, ghost_row(f, 1), u[-1])
            columns = [ghost_columns[pl.ds(start + 8 * j, 8), :] for j in range(height)]
            for j, value in enumerate(advance_tile(f, u, columns, False)):
                tile[f, 8 * j : 8 * j + 8, :] = value
        return carry

    def diffuse_merged(step, carry):
        read_ghosts(merged_line)
        ends = jnp.where(sub8 < 4, ghost_columns[8:16, :], ghost_columns[side : side + 8, :])
        for f in range(faces):
            for k in range(2):
                at = 16 * f + 8 * k
                u = strips[at : at + 8, :]
                strips[at : at + 8, :] = advance(
                    u, pltpu.roll(u, 1, 0), pltpu.roll(u, 7, 0),
                    ghost_row(f, 2 * k), ghost_row(f, 2 * k + 1), ends, 4 * f + 1 + 2 * k,
                )
        columns = [ghost_columns[pl.ds(start + 8 * j, 8), :] for j in range(height)]
        columns = columns[1:-1] + [jnp.where(sub8 < 4, columns[-1], columns[0])]
        for f in range(faces):
            u = [tile[f, 8 * j : 8 * j + 8, :] for j in range(1, height)]
            u[-1] = jnp.where(at_top, ghost_row(f, 0), u[-1])
            u[-1] = jnp.where(at_bottom, ghost_row(f, 1), u[-1])
            for j, value in enumerate(advance_tile(f, u, columns, True)):
                tile[f, 8 * j + 8 : 8 * j + 16, :] = value
        return carry

    lax.fori_loop(0, STEPS, diffuse, 0)

    receive_rows(lines_d)
    upper = sub < 4
    for f in range(faces):
        turn = (lambda v: v) if f % 2 == 0 else (lambda v: pltpu.roll(v, 4, 0))
        whole = [strips[32 * f + 8 * e : 32 * f + 8 * e + 8, :] for e in range(4)]
        edge_rows = jnp.where(upper, turn(first_d[f // 2]), turn(last_d[f // 2]))
        edge_columns = gather_strip(lambda s: packs[s, 2], f)
        strips[16 * f : 16 * f + 8, :] = edge_rows / jnp.where(upper, whole[0], whole[1])
        strips[16 * f + 8 : 16 * f + 16, :] = edge_columns / jnp.where(upper, whole[2], whole[3])
        around = jnp.where(upper, turn(below_d[f // 2]), turn(above_d[f // 2]))
        dual = density[f] / tile[f, 8 : 8 + rows, :]
        tile[f, 8 + rows :, :] = around / jnp.where(upper, tile[f, 8 + rows :, :], tile[f, :8, :])
        tile[f, 8 : 8 + rows, :] = dual
        results[1, f] = dual
    store_dual = pltpu.make_async_copy(results.at[1], out_hbm.at[1], local.at[2])
    store_dual.start()
    lax.fori_loop(0, STEPS, diffuse_merged, 0)

    marginal = scaling[...] * tile[:, 8 : 8 + rows, :]
    logs[...] = weight_ref[0] * jnp.log(marginal)

    def send_logs(i, slot):
        return remote(logs, others.at[slot], log_send.at[i], log_recv.at[slot], partners[i], "member")

    for i in range(members - 1):
        send_logs(i, m).start()
    weight = mine[...]
    for i in range(members - 1):
        send_weight(i, partners[i]).wait_recv()
        weight = weight + weights[partners[i]]
    if blocks > 1:
        weight = jnp.concatenate([weight] * blocks, axis=1)
    total = logs[...]
    for i in range(members - 1):
        send_logs(i, partners[i]).wait_recv()
        total = total + others[partners[i]]
    bary = jnp.exp(total / weight[:1].reshape(1, 1, side))
    results[2] = bary
    store_bary = pltpu.make_async_copy(results.at[2], out_hbm.at[2], local.at[1])
    store_bary.start()
    results[0] = (scaling[...] * bary) / marginal
    store_new = pltpu.make_async_copy(results.at[0], out_hbm.at[0], local.at[0])
    store_new.start()

    for i in range(members - 1):
        send_logs(i, m).wait_send()
        send_weight(i, m).wait_send()
    on_packs(send_pack, lambda copy: copy.wait_send(), False)
    on_rows(lines, lambda copy: copy.wait_send())
    on_rows(lines_d, lambda copy: copy.wait_send())
    store_dual.wait()
    store_bary.wait()
    store_new.wait()


def hand_out(results, new_hbm, dual_hbm, bary_hbm, held, loaded, stored):
    targets = (new_hbm.at[0], dual_hbm.at[0], bary_hbm)
    loads = [pltpu.make_async_copy(results.at[i], held.at[i], loaded.at[i]) for i in range(3)]
    stores = [pltpu.make_async_copy(held.at[i], targets[i], stored.at[i]) for i in range(3)]
    for load in loads:
        load.start()
    for load, store in zip(loads, stores):
        load.wait()
        store.start()
    for store in stores:
        store.wait()


def body(density, scaling, member_weights, seams):
    n = lax.axis_size("tile")
    members = lax.axis_size("member")
    _, faces, rows, side = scaling.shape
    vmem = lambda *shape: pltpu.VMEM(shape, jnp.float32)
    dma = lambda count: pltpu.SemaphoreType.DMA((count,))
    hbm = pl.BlockSpec(memory_space=pltpu.HBM)
    results = pl.pallas_call(
        functools.partial(kernel, n, members, faces, rows, side),
        out_shape=jax.ShapeDtypeStruct((3, faces, rows, side), jnp.float32),
        in_specs=[hbm] * 4,
        out_specs=hbm,
        scratch_shapes=[
            pltpu.SMEM(seams.shape, jnp.int32),
            pltpu.SMEM(member_weights.shape, jnp.float32),
            vmem(faces, rows, side),
            vmem(faces, rows, side),
            vmem(32 * faces, side),
            vmem(faces, rows + 16, side),
            vmem(32, side),
            vmem(side + 16, LANES),
            vmem(3, faces, rows, side),
            vmem(3, 8, LANES),
            vmem(n, 3, 8, LANES),
            *[vmem(faces, DEPTH, side)] * 4,
            *[vmem(faces // 2, 8, side)] * 6,
            vmem(faces, rows, side),
            vmem(members, faces, rows, side),
            vmem(8, LANES),
            vmem(members, 8, LANES),
            dma(5), dma(n), dma(n),
            dma(n + 1), dma(n + 1), dma(4), dma(n + 1), dma(n + 1), dma(4),
            dma(members), dma(members), dma(members), dma(members),
        ],
        compiler_params=pltpu.CompilerParams(
            collective_id=0, has_side_effects=True
        ),
    )(seams, member_weights, density, scaling)
    return pl.pallas_call(
        hand_out,
        out_shape=(
            jax.ShapeDtypeStruct(scaling.shape, jnp.float32),
            jax.ShapeDtypeStruct(scaling.shape, jnp.float32),
            jax.ShapeDtypeStruct(scaling.shape[1:], jnp.float32),
        ),
        in_specs=[hbm],
        out_specs=(hbm, hbm, hbm),
        scratch_shapes=[vmem(3, faces, rows, side), dma(3), dma(3)],
    )(results)


def solution(mesh):
    return jax.shard_map(
        body,
        mesh=mesh,
        in_specs=(
            P("member", None, "tile", None),
            P("member", None, "tile", None),
            P("member"),
            P(),
        ),
        out_specs=(
            P("member", None, "tile", None),
            P("member", None, "tile", None),
            P(None, "tile", None),
        ),
        check_vma=False,
    )
```

```python
import functools

import jax
import jax.numpy as jnp
from jax import lax
from jax.experimental import pallas as pl
from jax.experimental.pallas import tpu as pltpu
from jax.sharding import PartitionSpec as P

STEPS = 4
KAPPA = 0.24
LANES = 128
DEPTH = 8
MESH = pl.DeviceIdType.MESH


def kernel(
    n, members, faces, rows, side,
    seams_hbm, weight_hbm, density_hbm, scaling_hbm,
    out_hbm,
    seams_ref, weight_ref, density, scaling, strips, tile, ghosts, ghost_columns, results,
    pack, packs, first, last, above, below,
    top_d, bottom_d, first_d, last_d, above_d, below_d,
    logs, others, mine, weights,
    local, pack_send, pack_recv,
    top_send, bottom_send, row_recv, top_send_d, bottom_send_d, row_recv_d,
    log_send, log_recv, weight_send, weight_recv,
):
    t = lax.axis_index("tile")
    m = lax.axis_index("member")
    blocks = side // LANES
    per_block = LANES // rows
    pairs = faces // 2

    packs[...] = jnp.ones(packs.shape, jnp.float32)

    barrier = pltpu.get_barrier_semaphore()
    for i in range(1, n):
        pl.semaphore_signal(barrier, inc=1, device_id={"tile": lax.rem(t + i, n)}, device_id_type=MESH)
    for i in range(1, members):
        pl.semaphore_signal(
            barrier, inc=1, device_id={"member": lax.rem(m + i, members)}, device_id_type=MESH
        )
    load_scaling = pltpu.make_async_copy(scaling_hbm.at[0], scaling, local.at[0])
    load_density = pltpu.make_async_copy(density_hbm.at[0], density, local.at[1])
    load_scaling.start()
    load_density.start()
    load_weight = pltpu.make_async_copy(weight_hbm, weight_ref, local.at[3])
    load_seams = pltpu.make_async_copy(seams_hbm, seams_ref, local.at[4])
    load_weight.start()
    load_seams.start()

    sub8 = lax.broadcasted_iota(jnp.int32, (8, LANES), 0)
    lane8 = lax.broadcasted_iota(jnp.int32, (8, LANES), 1)
    sub = lax.broadcasted_iota(jnp.int32, (8, side), 0)
    lane = lax.broadcasted_iota(jnp.int32, (8, side), 1)

    def turned_columns(src, at):
        flat = src[:, :, at : at + LANES].reshape(faces * rows, LANES)
        rest = jnp.ones((LANES - faces * rows, LANES), jnp.float32)
        return jnp.concatenate([flat, rest], axis=0).T


    peers = [lax.rem(t + i, n) for i in range(1, n)]
    partners = [lax.rem(m + i, members) for i in range(1, members)]

    def remote(src, dst, send, recv, peer, axis="tile"):
        return pltpu.make_async_remote_copy(
            src_ref=src, dst_ref=dst, send_sem=send, recv_sem=recv,
            device_id={axis: peer}, device_id_type=MESH,
        )

    def send_pack(i, slot):
        return remote(pack, packs.at[slot], pack_send.at[i], pack_recv.at[slot], peers[i])

    def reaches(source, target):
        mirror = n - 1 - target
        ends = (target == 0) | (target == n - 1)
        return ends | (jnp.abs(source - target) <= 1) | (jnp.abs(source - mirror) <= 1)

    def on_packs(sends, act, arriving):
        for i in range(n - 1):

            @pl.when(reaches(peers[i], t) if arriving else reaches(t, peers[i]))
            def _():
                act(sends(i, peers[i] if arriving else t))

    def row_sends(top, bottom, first, last, above, below, top_send, bottom_send, recv):
        up_peer, down_peer = lax.rem(t + n - 1, n), lax.rem(t + 1, n)
        return (
            [remote(top, first, top_send.at[i], recv.at[0], p) for i, p in enumerate(peers)],
            [remote(bottom, last, bottom_send.at[i], recv.at[1], p) for i, p in enumerate(peers)],
            remote(top, below, top_send.at[n], recv.at[2], up_peer),
            remote(bottom, above, bottom_send.at[n], recv.at[3], down_peer),
        )

    lines = row_sends(
        scaling.at[:, pl.ds(0, DEPTH), :], scaling.at[:, pl.ds(rows - DEPTH, DEPTH), :],
        first, last, above, below, top_send, bottom_send, row_recv,
    )
    lines_d = row_sends(
        top_d, bottom_d, first_d, last_d, above_d, below_d, top_send_d, bottom_send_d, row_recv_d
    )

    def on_rows(sends, act):
        to_first, to_last, to_above, to_below = sends

        @pl.when(t == 0)
        def _():
            for copy in reversed(to_first):
                act(copy)

        @pl.when(t == n - 1)
        def _():
            for copy in to_last:
                act(copy)

        @pl.when(t > 0)
        def _():
            act(to_above)

        @pl.when(t < n - 1)
        def _():
            act(to_below)

    def receive_rows(sends):
        to_first, to_last, to_above, to_below = sends

        @pl.when(t > 0)
        def _():
            to_first[0].wait_recv()
            to_below.wait_recv()

        @pl.when(t < n - 1)
        def _():
            to_last[0].wait_recv()
            to_above.wait_recv()

    load_scaling.wait()
    turned = turned_columns(scaling, 0)
    pack[0] = turned[:8]
    pack[1] = (turned if blocks == 1 else turned_columns(scaling, side - LANES))[LANES - 8 :]
    load_density.wait()
    turned = turned_columns(density, 0)
    other = turned if blocks == 1 else turned_columns(density, side - LANES)
    pack[2] = jnp.where(sub8 < 4, turned[:8], other[LANES - 8 :])
    packs[t] = pack[...]
    for j in range(pairs):
        top_d[j] = jnp.where(
            sub < 4, density[2 * j, :8, :], pltpu.roll(density[2 * j + 1, :8, :], 4, 0)
        )
        bottom_d[j] = jnp.where(
            sub >= 4, density[2 * j, rows - 8 :, :], pltpu.roll(density[2 * j + 1, rows - 8 :, :], 4, 0)
        )
    pl.semaphore_wait(barrier, n - 1 + members - 1)

    on_packs(send_pack, lambda copy: copy.start(), False)
    on_rows(lines, lambda copy: copy.start())

    on_rows(lines_d, lambda copy: copy.start())

    def send_weight(i, slot):
        return remote(
            mine, weights.at[slot], weight_send.at[i], weight_recv.at[slot], partners[i], "member"
        )

    load_weight.wait()
    mine[...] = jnp.full((8, LANES), weight_ref[0], jnp.float32)
    for i in range(members - 1):
        send_weight(i, m).start()

    @pl.when(t == 0)
    def _():
        first[...] = scaling[:, :DEPTH, :]
        first_d[...] = top_d[...]
        above[...] = jnp.ones(above.shape, jnp.float32)
        above_d[...] = jnp.ones(above_d.shape, jnp.float32)

    @pl.when(t == n - 1)
    def _():
        last[...] = scaling[:, rows - DEPTH :, :]
        last_d[...] = bottom_d[...]
        below[...] = jnp.ones(below.shape, jnp.float32)
        below_d[...] = jnp.ones(below_d.shape, jnp.float32)

    ghosts[...] = jnp.zeros(ghosts.shape, jnp.float32)
    ghost_columns[...] = jnp.zeros(ghost_columns.shape, jnp.float32)

    load_seams.wait()
    whole_line, merged_line = {}, {}
    row_of = lax.broadcasted_iota(jnp.int32, (24, LANES), 0)
    flipped = jnp.zeros((24, LANES), jnp.int32)
    for f in range(faces):
        for e in range(4):
            face, edge = seams_ref[0, e, f], seams_ref[1, e, f]
            second = lax.rem(edge, 2)
            whole_line[f, e] = 32 * face + 8 * edge + 7 * second
            merged_line[f, e] = 16 * face + 4 * (edge - second) + 7 * second
            flipped = jnp.where(row_of == 4 * f + 3 - e, seams_ref[2, e, f], flipped)
    turns = flipped == 1

    def gather_strip(read, f):
        parts = []
        for b in range(blocks):
            out = jnp.ones((8, LANES), jnp.float32)
            for k in range(per_block):
                shift = (rows * (k - f)) % LANES
                piece = read(b * per_block + k)
                piece = pltpu.roll(piece, shift, 1) if shift else piece
                out = jnp.where((lane8 >= rows * k) & (lane8 < rows * (k + 1)), piece, out)
            parts.append(out)
        return parts[0] if blocks == 1 else jnp.concatenate(parts, axis=1)

    on_packs(send_pack, lambda copy: copy.wait_recv(), True)
    for f in range(faces):
        for k in range(2):
            at = 32 * f + 16 + 8 * k
            strips[at : at + 8, :] = gather_strip(lambda s: packs[s, k], f)
    receive_rows(lines)
    for f in range(faces):
        strips[32 * f : 32 * f + 8, :] = first[f]
        strips[32 * f + 8 : 32 * f + 16, :] = last[f]
        tile[f, :8] = above[f]
        tile[f, 8 : 8 + rows] = scaling[f]
        tile[f, 8 + rows :] = below[f]

    start = pl.multiple_of(rows * t, 8)
    reverse = LANES - 1 - lane8
    at_top = (sub == 7) & (t == 0)
    at_bottom = (sub == 0) & (t == n - 1)
    height = (rows + 16) // 8

    def place(line, shift):
        line = pltpu.roll(line, (LANES - shift) % LANES, 1)
        return line if blocks == 1 else jnp.concatenate([line] * blocks, axis=1)

    def stencil(u, up, down, ends):
        left = jnp.where(lane == 0, ends, pltpu.roll(u, 1, 1))
        right = jnp.where(lane == side - 1, ends, pltpu.roll(u, side - 1, 1))
        return u + KAPPA * (((up + down) + (left + right)) - 4.0 * u)

    def read_ghosts(line_of):
        for f in range(faces):
            for e in range(4):
                row = 4 * f + 3 - e
                ghosts[row : row + 1, :] = strips[pl.ds(line_of[f, e], 1), :]
        lines = [ghosts[: 4 * faces, b * LANES : (b + 1) * LANES] for b in range(blocks)]
        rest = jnp.zeros((32 - 4 * faces, LANES), jnp.float32)
        for b in range(blocks):
            backward = jnp.concatenate(
                [
                    jnp.take_along_axis(
                        lines[blocks - 1 - b][r : r + 8], reverse, axis=1, mode="promise_in_bounds"
                    )
                    for r in range(0, 4 * faces, 8)
                ],
                axis=0,
            )
            line = jnp.where(turns, backward, lines[b])
            ghosts[: 4 * faces, b * LANES : (b + 1) * LANES] = line
            at = 8 + b * LANES
            ghost_columns[at : at + LANES, :32] = jnp.concatenate([line, rest], axis=0).T

    def ghost_row(f, e):
        row = 4 * f + 3 - e
        return jnp.broadcast_to(ghosts[row : row + 1, :], (8, side))

    def advance(u, first_rows, last_rows, over, under, columns, shift):
        up, down = first_rows, last_rows
        if over is not None:
            up = jnp.where(sub == 0, over, up)
        if under is not None:
            down = jnp.where(sub == 7, under, down)
        return stencil(u, up, down, place(columns, shift))

    def advance_tile(f, u, columns, closed):
        count = len(u)
        ups = [pltpu.roll(v, 1, 0) for v in u]
        downs = [pltpu.roll(v, 7, 0) for v in u]
        result = []
        for j in range(count):
            before = ups[j - 1] if j or closed else None
            after = downs[(j + 1) % count] if j < count - 1 or closed else None
            result.append(advance(u[j], ups[j], downs[j], before, after, columns[j], 4 * f + 1))
        return result

    def diffuse(step, carry):
        read_ghosts(whole_line)
        ends = (ghost_columns[8:16, :], ghost_columns[side : side + 8, :])
        for f in range(faces):
            for e in range(4):
                at = 32 * f + 8 * e
                u = strips[at : at + 8, :]
                ghost = ghost_row(f, e)
                over, under = (None, ghost) if e % 2 else (ghost, None)
                strips[at : at + 8, :] = advance(
                    u, pltpu.roll(u, 1, 0), pltpu.roll(u, 7, 0), over, under,
                    ends[e % 2], 4 * f + 1 + (e // 2) * 2,
                )
        for f in range(faces):
            u = [tile[f, 8 * j : 8 * j + 8, :] for j in range(height)]
            u[0] = jnp.where(at_top, ghost_row(f, 0), u[0])
            u[-1] = jnp.where(at_bottom, ghost_row(f, 1), u[-1])
            columns = [ghost_columns[pl.ds(start + 8 * j, 8), :] for j in range(height)]
            for j, value in enumerate(advance_tile(f, u, columns, False)):
                tile[f, 8 * j : 8 * j + 8, :] = value
        return carry

    def diffuse_merged(step, carry):
        read_ghosts(merged_line)
        ends = jnp.where(sub8 < 4, ghost_columns[8:16, :], ghost_columns[side : side + 8, :])
        for f in range(faces):
            for k in range(2):
                at = 16 * f + 8 * k
                u = strips[at : at + 8, :]
                strips[at : at + 8, :] = advance(
                    u, pltpu.roll(u, 1, 0), pltpu.roll(u, 7, 0),
                    ghost_row(f, 2 * k), ghost_row(f, 2 * k + 1), ends, 4 * f + 1 + 2 * k,
                )
        columns = [ghost_columns[pl.ds(start + 8 * j, 8), :] for j in range(height)]
        columns = columns[1:-1] + [jnp.where(sub8 < 4, columns[-1], columns[0])]
        for f in range(faces):
            u = [tile[f, 8 * j : 8 * j + 8, :] for j in range(1, height)]
            u[-1] = jnp.where(at_top, ghost_row(f, 0), u[-1])
            u[-1] = jnp.where(at_bottom, ghost_row(f, 1), u[-1])
            for j, value in enumerate(advance_tile(f, u, columns, True)):
                tile[f, 8 * j + 8 : 8 * j + 16, :] = value
        return carry

    lax.fori_loop(0, STEPS, diffuse, 0, unroll=2)

    receive_rows(lines_d)
    upper = sub < 4
    for f in range(faces):
        turn = (lambda v: v) if f % 2 == 0 else (lambda v: pltpu.roll(v, 4, 0))
        whole = [strips[32 * f + 8 * e : 32 * f + 8 * e + 8, :] for e in range(4)]
        edge_rows = jnp.where(upper, turn(first_d[f // 2]), turn(last_d[f // 2]))
        edge_columns = gather_strip(lambda s: packs[s, 2], f)
        strips[16 * f : 16 * f + 8, :] = edge_rows / jnp.where(upper, whole[0], whole[1])
        strips[16 * f + 8 : 16 * f + 16, :] = edge_columns / jnp.where(upper, whole[2], whole[3])
        around = jnp.where(upper, turn(below_d[f // 2]), turn(above_d[f // 2]))
        dual = density[f] / tile[f, 8 : 8 + rows, :]
        tile[f, 8 + rows :, :] = around / jnp.where(upper, tile[f, 8 + rows :, :], tile[f, :8, :])
        tile[f, 8 : 8 + rows, :] = dual
        results[1, f] = dual
    store_dual = pltpu.make_async_copy(results.at[1], out_hbm.at[1], local.at[2])
    store_dual.start()
    lax.fori_loop(0, STEPS, diffuse_merged, 0, unroll=2)

    marginal = scaling[...] * tile[:, 8 : 8 + rows, :]
    logs[...] = weight_ref[0] * jnp.log(marginal)

    def send_logs(i, slot):
        return remote(logs, others.at[slot], log_send.at[i], log_recv.at[slot], partners[i], "member")

    for i in range(members - 1):
        send_logs(i, m).start()
    weight = mine[...]
    for i in range(members - 1):
        send_weight(i, partners[i]).wait_recv()
        weight = weight + weights[partners[i]]
    if blocks > 1:
        weight = jnp.concatenate([weight] * blocks, axis=1)
    total = logs[...]
    for i in range(members - 1):
        send_logs(i, partners[i]).wait_recv()
        total = total + others[partners[i]]
    bary = jnp.exp(total / weight[:1].reshape(1, 1, side))
    results[2] = bary
    store_bary = pltpu.make_async_copy(results.at[2], out_hbm.at[2], local.at[1])
    store_bary.start()
    results[0] = (scaling[...] * bary) / marginal
    store_new = pltpu.make_async_copy(results.at[0], out_hbm.at[0], local.at[0])
    store_new.start()

    for i in range(members - 1):
        send_logs(i, m).wait_send()
        send_weight(i, m).wait_send()
    on_packs(send_pack, lambda copy: copy.wait_send(), False)
    on_rows(lines, lambda copy: copy.wait_send())
    on_rows(lines_d, lambda copy: copy.wait_send())
    store_dual.wait()
    store_bary.wait()
    store_new.wait()


def hand_out(results, new_hbm, dual_hbm, bary_hbm, held, loaded, stored):
    targets = (new_hbm.at[0], dual_hbm.at[0], bary_hbm)
    loads = [pltpu.make_async_copy(results.at[i], held.at[i], loaded.at[i]) for i in range(3)]
    stores = [pltpu.make_async_copy(held.at[i], targets[i], stored.at[i]) for i in range(3)]
    for load in loads:
        load.start()
    for load, store in zip(loads, stores):
        load.wait()
        store.start()
    for store in stores:
        store.wait()


def body(density, scaling, member_weights, seams):
    n = lax.axis_size("tile")
    members = lax.axis_size("member")
    _, faces, rows, side = scaling.shape
    vmem = lambda *shape: pltpu.VMEM(shape, jnp.float32)
    dma = lambda count: pltpu.SemaphoreType.DMA((count,))
    hbm = pl.BlockSpec(memory_space=pltpu.HBM)
    results = pl.pallas_call(
        functools.partial(kernel, n, members, faces, rows, side),
        out_shape=jax.ShapeDtypeStruct((3, faces, rows, side), jnp.float32),
        in_specs=[hbm] * 4,
        out_specs=hbm,
        scratch_shapes=[
            pltpu.SMEM(seams.shape, jnp.int32),
            pltpu.SMEM(member_weights.shape, jnp.float32),
            vmem(faces, rows, side),
            vmem(faces, rows, side),
            vmem(32 * faces, side),
            vmem(faces, rows + 16, side),
            vmem(32, side),
            vmem(side + 16, LANES),
            vmem(3, faces, rows, side),
            vmem(3, 8, LANES),
            vmem(n, 3, 8, LANES),
            *[vmem(faces, DEPTH, side)] * 4,
            *[vmem(faces // 2, 8, side)] * 6,
            vmem(faces, rows, side),
            vmem(members, faces, rows, side),
            vmem(8, LANES),
            vmem(members, 8, LANES),
            dma(5), dma(n), dma(n),
            dma(n + 1), dma(n + 1), dma(4), dma(n + 1), dma(n + 1), dma(4),
            dma(members), dma(members), dma(members), dma(members),
        ],
        compiler_params=pltpu.CompilerParams(
            collective_id=0, has_side_effects=True
        ),
    )(seams, member_weights, density, scaling)
    return pl.pallas_call(
        hand_out,
        out_shape=(
            jax.ShapeDtypeStruct(scaling.shape, jnp.float32),
            jax.ShapeDtypeStruct(scaling.shape, jnp.float32),
            jax.ShapeDtypeStruct(scaling.shape[1:], jnp.float32),
        ),
        in_specs=[hbm],
        out_specs=(hbm, hbm, hbm),
        scratch_shapes=[vmem(3, faces, rows, side), dma(3), dma(3)],
    )(results)


def solution(mesh):
    return jax.shard_map(
        body,
        mesh=mesh,
        in_specs=(
            P("member", None, "tile", None),
            P("member", None, "tile", None),
            P("member"),
            P(),
        ),
        out_specs=(
            P("member", None, "tile", None),
            P("member", None, "tile", None),
            P(None, "tile", None),
        ),
        check_vma=False,
    )
```
